256 devices in a mesh: seq: 32 (over z, x), head: 8 (over y, core).
Axes of the slice: x: 4, y: 4, z: 8, core: 2. Of those that a mesh axis runs over, the one named last changes fastest.
Arguments:
- embedding: bfloat16 [8192, 4096], P('seq', 'head'), may hold values from -6 to 6
- noise_draw: bfloat16 [8192, 4096], P('seq', 'head'), may hold values from -3 to 3
- weight_x: bfloat16 [4096, 4096], P(None, 'head'), may hold values from -0.09375 to 0.09375
- weight_z: bfloat16 [4096, 4096], P(None, 'head'), may hold values from -0.09375 to 0.09375
- b_proj: float32 [8192, 128], P('seq'), may hold values from -0.015625 to 0.015625
- c_proj: float32 [8192, 128], P('seq'), may hold values from -6 to 6
- log_decay: float32 [64, 8192], P('head', 'seq'), may hold values from -1.3 to 0, as said below
- skip_gain: float32 [64], P('head'), may hold values from 0.5 to 1.5
- class_weight: bfloat16 [4096, 32], P('head'), may hold values from -6 to 6
- true_label: int32 [8192], P('seq'), may hold values from 0 to 31
Outputs:
- emb_grad: float32 [8192, 4096], P('seq', 'head')
The draws below stay inside these ranges and needn't reach their ends.
Inputs may be any that keep to these rules, and one draw needn't show every extreme that they name: `log_decay`: each entry is the logarithm of one head's decay factor at one token.
All inputs are finite; a program needn't handle non-finite values.
Results may differ from the reference program's by a relative error of at most 0.02.
Values may be sent and summed in bfloat16 or wider, within the bound.
A program may use at most 128 MiB of HBM per device.

```python
import math
import jax
import jax.numpy as jnp
from jax import lax

D = 4096
HEAD_TOTAL = 64
P_SIZE = 64
N = 128
SPAN = 256
CLASSES = 32
TOK_DEV = 256
DOCUMENT_TOKENS = 8192
N_HEAD = 8


def draw_log_decay(key, part):
    key = jax.random.fold_in(key, 11)
    random_child_keys = jax.random.split(key, 11)
    fast_fraction = 0.3
    spike_fraction = 0.4
    selector_key = jax.random.uniform(random_child_keys[0], (HEAD_TOTAL, 1))
    quick_rate = jnp.exp(jax.random.uniform(random_child_keys[1], (HEAD_TOTAL, 1), minval=math.log(1.0 / 50.0), maxval=math.log(1.0 / 30.0)))
    slow_rate = jnp.exp(jax.random.uniform(random_child_keys[2], (HEAD_TOTAL, 1), minval=math.log(0.01), maxval=math.log(0.3))) / DOCUMENT_TOKENS
    is_quick = selector_key < fast_fraction
    has_spikes = jnp.logical_and(selector_key >= fast_fraction, selector_key < fast_fraction + spike_fraction)
    decay_factors = jnp.where(is_quick, quick_rate, slow_rate)
    number_of_blocks = DOCUMENT_TOKENS // TOK_DEV
    device_multiplier = jnp.exp(jax.random.uniform(random_child_keys[3], (HEAD_TOTAL, number_of_blocks, 1), minval=math.log(0.5), maxval=math.log(1.5)))
    device_multiplier = jnp.broadcast_to(device_multiplier, (HEAD_TOTAL, number_of_blocks, TOK_DEV)).reshape(HEAD_TOTAL, DOCUMENT_TOKENS)
    noise_level = jax.random.uniform(random_child_keys[4], (HEAD_TOTAL, DOCUMENT_TOKENS), minval=0.25, maxval=1.75)
    spike_locations = jax.random.randint(random_child_keys[5], (2,), 0, DOCUMENT_TOKENS)
    spike_retain = jax.random.uniform(random_child_keys[6], (2,), minval=0.55, maxval=0.8)
    token_places = jnp.arange(DOCUMENT_TOKENS)
    spike_events = token_places[None, :] == spike_locations[:, None]
    spike_log_value = jnp.sum(jnp.where(spike_events, jnp.log(spike_retain)[:, None], 0.0), axis=0)
    window_len = max(TOK_DEV // 8, 2)
    half_window = window_len // 2
    spike_block = jax.random.uniform(random_child_keys[7], (HEAD_TOTAL, number_of_blocks, 1)) < 0.5
    leading_position = TOK_DEV - 1 - jax.random.randint(random_child_keys[8], (HEAD_TOTAL, number_of_blocks, 1), 0, half_window)
    trailing_position = TOK_DEV - 1 - half_window - jax.random.randint(random_child_keys[9], (HEAD_TOTAL, number_of_blocks, 1), 0, half_window)
    noise_strength = jax.random.uniform(random_child_keys[10], (HEAD_TOTAL, number_of_blocks, 2), minval=-1.3, maxval=-1.1)
    local_positions = jnp.arange(TOK_DEV)[None, None, :]
    spike_magnitude = jnp.where(local_positions == leading_position, noise_strength[:, :, 0:1], 0.0)
    spike_magnitude = spike_magnitude + jnp.where(local_positions == trailing_position, noise_strength[:, :, 1:2], 0.0)
    spike_active = jnp.logical_and(has_spikes[:, :, None], spike_block)
    spike_magnitude = jnp.where(spike_active, spike_magnitude, 0.0).reshape(HEAD_TOTAL, DOCUMENT_TOKENS)
    grand_total = -decay_factors * device_multiplier * noise_level + spike_log_value[None, :] + spike_magnitude
    return jnp.maximum(grand_total, -1.3).astype(jnp.float32)


def set_ends(result, rng, least, largest):
    spot = [jax.random.randint(jax.random.fold_in(rng, axis), (), 0, length) for axis, length in enumerate(result.shape)]
    main_axis = result.shape.index(max(result.shape))
    next_to = spot[:main_axis] + [(spot[main_axis] + 1) % result.shape[main_axis]] + spot[main_axis + 1:]
    return result.at[tuple(spot)].set(least).at[tuple(next_to)].set(largest)


def shard_levels(key, shape, cuts, low, high):
    def one(dim, shards_of):
        draws = jax.random.uniform(jax.random.fold_in(jax.random.fold_in(key, 6), dim), (shards_of,), jnp.float32, low / len(cuts), high / len(cuts))
        return jnp.repeat(jnp.exp(draws), shape[dim] // shards_of).reshape((-1,) + (1,) * (len(shape) - dim - 1))

    factor_of = one(*cuts[0])
    for cut in cuts[1:]:
        factor_of = factor_of * one(*cut)
    return factor_of


def normal_values(key, shape, scale, most, cuts=(), held_as=jnp.bfloat16):
    values = jax.random.normal(key, shape, jnp.float32) * scale
    if len(cuts) > 0:
        values = shard_levels(key, shape, cuts, -0.22, 0.18) * values
    return jnp.clip(values, min=-most, max=most).astype(held_as)


def setup_inputs(seed: int = 0) -> dict:
    key_list = jax.random.split(jax.random.key(seed), 11)
    return {
        "embedding": normal_values(key_list[0], (DOCUMENT_TOKENS, D), 1.0, 6.0, ((0, 32), (1, 8))),
        "noise_draw": normal_values(key_list[1], (DOCUMENT_TOKENS, D), 0.5, 3.0, ((0, 32), (1, 8))),
        "weight_x": normal_values(key_list[2], (D, HEAD_TOTAL * P_SIZE), D ** -0.5, 0.09375, ((1, 8),)),
        "weight_z": normal_values(key_list[3], (D, HEAD_TOTAL * P_SIZE), D ** -0.5, 0.09375, ((1, 8),)),
        "b_proj": normal_values(key_list[4], (DOCUMENT_TOKENS, N), (N * DOCUMENT_TOKENS // 9) ** -0.5, 0.015625, ((0, 32),), jnp.float32),
        "c_proj": normal_values(key_list[5], (DOCUMENT_TOKENS, N), 1 ** -0.5, 6.0, ((0, 32),), jnp.float32),
        "log_decay": draw_log_decay(jax.random.fold_in(key_list[10], 71), 0),
        "skip_gain": jnp.clip(0.5 + 1.0 * jax.random.uniform(key_list[7], (HEAD_TOTAL,), jnp.float32) ** shard_levels(key_list[7], (HEAD_TOTAL,), ((0, 8),), -0.2, 0.2), 0.5, 1.5),
        "class_weight": normal_values(key_list[8], (HEAD_TOTAL * P_SIZE, CLASSES), 1 ** -0.5, 6.0, ((0, 8),)),
        "true_label": set_ends(jax.random.randint(key_list[9], (DOCUMENT_TOKENS,), 0, CLASSES), jax.random.fold_in(key_list[9], 1), 0, CLASSES - 1).astype(jnp.int32),
    }


precise = lax.Precision.HIGHEST


def span_weights(local_cum, c_block, b_block):
    scores = jnp.einsum('tn,sn->ts', c_block, b_block, precision=precise)
    cum_heads = local_cum.T
    spread = cum_heads[:, :, None] - cum_heads[:, None, :]
    block_width = local_cum.shape[0]
    lower = jnp.arange(block_width)[:, None] >= jnp.arange(block_width)[None, :]
    return jnp.where(lower[None, :, :], jnp.exp(jnp.minimum(spread, 0.0)), 0.0) * scores[None, :, :]


def local_forward(values, log_rates, b_rows, c_rows, block_width, start_state):
    length, head_count, head_dim = values.shape
    number_of_blocks = length // block_width
    blocks = (values.reshape(number_of_blocks, block_width, head_count, head_dim),
              log_rates.reshape(number_of_blocks, block_width, head_count),
              b_rows.reshape(number_of_blocks, block_width, b_rows.shape[1]),
              c_rows.reshape(number_of_blocks, block_width, c_rows.shape[1]))

    def block_step(carried, block_data):
        x_block, rate_block, b_block, c_block = block_data
        local_cum = jnp.cumsum(rate_block, axis=0)
        weights = span_weights(local_cum, c_block, b_block)
        output = jnp.einsum('hts,shp->thp', weights, x_block, precision=precise)
        output = output + jnp.exp(local_cum)[:, :, None] * jnp.einsum('tn,hpn->thp', c_block, carried, precision=precise)
        final_cum = local_cum[-1]
        carried = jnp.exp(final_cum)[:, None, None] * carried + jnp.einsum(
            'sh,shp,sn->hpn', jnp.exp(final_cum[None, :] - local_cum), x_block, b_block, precision=precise)
        return carried, output

    carried, outputs = lax.scan(block_step, start_state, blocks)
    return carried, outputs.reshape(length, head_count, head_dim)


def local_backward(grads, log_rates, b_rows, c_rows, block_width, start_state):
    length, head_count, head_dim = grads.shape
    number_of_blocks = length // block_width
    blocks = (grads.reshape(number_of_blocks, block_width, head_count, head_dim),
              log_rates.reshape(number_of_blocks, block_width, head_count),
              b_rows.reshape(number_of_blocks, block_width, b_rows.shape[1]),
              c_rows.reshape(number_of_blocks, block_width, c_rows.shape[1]))

    def block_step(carried, block_data):
        g_block, rate_block, b_block, c_block = block_data
        local_cum = jnp.cumsum(rate_block, axis=0)
        weights = span_weights(local_cum, c_block, b_block)
        final_cum = local_cum[-1]
        output = jnp.einsum('hts,thp->shp', weights, g_block, precision=precise)
        output = output + jnp.exp(final_cum[None, :] - local_cum)[:, :, None] * jnp.einsum(
            'sn,hpn->shp', b_block, carried, precision=precise)
        carried = jnp.exp(final_cum)[:, None, None] * carried + jnp.einsum(
            'th,thp,tn->hpn', jnp.exp(local_cum), g_block, c_block, precision=precise)
        return carried, output

    carried, outputs = lax.scan(block_step, start_state, blocks, reverse=True)
    return carried, outputs.reshape(length, head_count, head_dim)


def reference(embedding, noise_draw, weight_x, weight_z, b_proj, c_proj, log_decay, skip_gain, class_weight, true_label):
    mixed = (embedding.astype(jnp.float32) + noise_draw.astype(jnp.float32)).astype(jnp.bfloat16)
    x_inner = jnp.dot(mixed, weight_x, preferred_element_type=jnp.float32)
    z_inner = jnp.dot(mixed, weight_z, preferred_element_type=jnp.float32)
    rates_tok = log_decay.T
    x_heads = x_inner.reshape(DOCUMENT_TOKENS, HEAD_TOTAL, P_SIZE)
    start_zero = jnp.zeros((HEAD_TOTAL, P_SIZE, N), jnp.float32)
    unused, scanned = local_forward(x_heads, rates_tok, b_proj, c_proj, SPAN, start_zero)
    output_y = (scanned + skip_gain[None, :, None] * x_heads).reshape(DOCUMENT_TOKENS, HEAD_TOTAL * P_SIZE)
    columns = jnp.take(class_weight.astype(jnp.float32).T, true_label.astype(jnp.int32), axis=0)
    sigmoid_z = jax.nn.sigmoid(z_inner)
    grad_y = columns * (z_inner * sigmoid_z)
    grad_z = (columns * output_y * sigmoid_z * (1.0 + z_inner * (1.0 - sigmoid_z))).astype(jnp.bfloat16)
    grad_heads = grad_y.reshape(DOCUMENT_TOKENS, HEAD_TOTAL, P_SIZE)
    unused_grad, back = local_backward(grad_heads, rates_tok, b_proj, c_proj, SPAN, start_zero)
    grad_x = (back + skip_gain[None, :, None] * grad_heads).reshape(DOCUMENT_TOKENS, HEAD_TOTAL * P_SIZE).astype(jnp.bfloat16)
    group_width = HEAD_TOTAL * P_SIZE // N_HEAD
    summed = jnp.zeros((DOCUMENT_TOKENS, D), jnp.float32)
    for group_index in range(N_HEAD):
        first_column = group_index * group_width
        last_column = first_column + group_width
        partial_value = jnp.dot(grad_x[:, first_column:last_column], weight_x[:, first_column:last_column].T,
                          preferred_element_type=jnp.float32)
        partial_value = partial_value + jnp.dot(grad_z[:, first_column:last_column], weight_z[:, first_column:last_column].T,
                                    preferred_element_type=jnp.float32)
        rounded = lax.optimization_barrier(partial_value.astype(jnp.bfloat16))
        summed = summed + rounded.astype(jnp.float32)
    return summed
```

```python
import functools

import jax
import jax.numpy as jnp
from jax import lax
from jax.experimental import pallas as pl
from jax.experimental.pallas import tpu as pltpu
from jax.sharding import PartitionSpec as P

F32 = jnp.float32
BF16 = jnp.bfloat16
MESH = pl.DeviceIdType.MESH
NX = 4
PRECISE = lax.Precision.HIGHEST
LO, HI = 0, 1


def dot(a, b):
    return jnp.dot(a, b, preferred_element_type=F32)


def dot_t(a, b, precision=None):
    return lax.dot_general(
        a, b, (((1,), (1,)), ((), ())), preferred_element_type=F32, precision=precision
    )


class Links:
    def __init__(self, send_sems, recv_sems):
        self.send_sems, self.recv_sems = send_sems, recv_sems
        self.sent = []

    def make(self, k, src, dst, device):
        return pltpu.make_async_remote_copy(
            src_ref=src,
            dst_ref=dst,
            send_sem=self.send_sems.at[k],
            recv_sem=self.recv_sems.at[k],
            device_id=device,
            device_id_type=MESH,
        )

    def send(self, k, src, dst, device):
        copy = self.make(k, src, dst, device)
        copy.start()
        self.sent.append(copy)

    def arrive(self, k, dst, device):
        self.make(k, dst, dst, device).wait_recv()

    def finish(self):
        for copy in self.sent:
            copy.wait_send()


def kernel(
    nz,
    ny,
    emb_h,
    noise_h,
    wx_h,
    wz_h,
    b_h,
    c_h,
    ld_h,
    cw_h,
    lab_h,
    skip_s,
    out_h,
    ev,
    nv,
    wx,
    wz,
    bv,
    cv,
    ldv,
    cwv,
    labv,
    mix,
    acc,
    dec_in,
    dec_out,
    cols,
    wts,
    wts_t,
    b_t,
    c_t,
    tots,
    tots_x,
    group,
    groups,
    f_send,
    b_send,
    f_x,
    b_x,
    f_pre,
    b_pre,
    f_tot,
    b_tot,
    t_z,
    f_back,
    b_back,
    f_in,
    b_in,
    y_loc,
    gx_loc,
    fz,
    gx,
    gz,
    s_sib,
    r_sib,
    cs_opp,
    r_lo,
    r_hi,
    cs_r,
    cs_l,
    s_right,
    s_left,
    r_left,
    r_right,
    outv,
    local_sems,
    send_sems,
    recv_sems,
):
    tok, feat = ev.shape
    half = tok // 2
    width = acc.shape[1] // 2
    heads = ldv.shape[0]
    head_dim = width // heads
    state = bv.shape[1]
    lanes = width // NX
    seq, head = lax.axis_index("seq"), lax.axis_index("head")
    z, x = seq // NX, seq % NX
    y, core = head // 2, head % 2
    other = 1 - 2 * core

    links = Links(send_sems, recv_sems)
    counter = [0]

    def new(count=1):
        first = counter[0]
        counter[0] += count
        return first

    pairs = [
        (emb_h, ev),
        (noise_h, nv),
        (ld_h, ldv),
        (b_h, bv),
        (c_h, cv),
        (cw_h, cwv),
        (lab_h, labv),
        (wx_h, wx),
        (wz_h, wz),
    ]
    loads = [pltpu.make_async_copy(s, d, local_sems.at[i]) for i, (s, d) in enumerate(pairs)]
    for load in loads:
        load.start()

    sib = {"head": head + other}
    blk_r = ((y + 1) % ny) * 2 + core
    blk_l = ((y + ny - 1) % ny) * 2 + core
    blk_o = ((y + 2) % ny) * 2 + core
    right, left = {"head": blk_r}, {"head": blk_l}

    def at_x(d):
        return (x + d) % NX

    def at_z(d):
        return (z + d) % nz

    def dev_x(d):
        return {"seq": z * NX + at_x(d)}

    def dev_z(d):
        return {"seq": at_z(d) * NX + x}

    barrier = pltpu.get_barrier_semaphore()
    partners = [sib, right, left]
    partners += [dev_x(d) for d in range(1, NX)] + [dev_z(d) for d in range(1, nz)]
    for partner in partners:
        pl.semaphore_signal(barrier, inc=1, device_id=partner, device_id_type=MESH)

    loads[0].wait()
    loads[1].wait()
    mix[head] = (ev[...].astype(F32) + nv[...].astype(F32)).astype(BF16)
    pl.semaphore_wait(barrier, len(partners))

    part = (pl.ds(0, half), pl.ds(half, half))

    def piece(blk, h):
        return mix.at[blk, part[h]]

    k_r, k_l, k_own = new(2), new(2), new()
    k_fr, k_fl = new(), new()
    k_sib = {name: new(2) for name in ("l", "r", "o")}

    def hand_on(name, blk, h):
        links.send(k_sib[name] + h, piece(blk, h), piece(blk, h), sib)

    def from_sib(name, blk):
        for h in (LO, HI):
            links.arrive(k_sib[name] + h, piece(blk, h), sib)

    links.send(k_r + LO, piece(head, LO), piece(head, LO), right)
    links.send(k_l + HI, piece(head, HI), piece(head, HI), left)
    links.send(k_own, mix.at[head], mix.at[head], sib)
    links.send(k_r + HI, piece(head, HI), piece(head, HI), right)
    links.send(k_l + LO, piece(head, LO), piece(head, LO), left)

    loads[2].wait()
    rates = ldv[...]
    ones_t = lax.broadcasted_iota(jnp.int32, (tok, tok), 0)
    ones_s = lax.broadcasted_iota(jnp.int32, (tok, tok), 1)
    lower = ones_t >= ones_s
    tri = jnp.where(lower, 1.0, 0.0).astype(F32)
    tri_t = jnp.where(ones_s >= ones_t, 1.0, 0.0).astype(F32)
    cum_row = jnp.dot(rates, tri_t, preferred_element_type=F32, precision=PRECISE)
    wide = jnp.concatenate(
        [jnp.broadcast_to(rates[h : h + 1, :], (head_dim, tok)) for h in range(heads)], axis=0
    )
    cum = dot_t(tri, wide, PRECISE)
    total = cum[tok - 1 : tok, :]
    dec_in[...] = jnp.exp(cum)
    dec_out[...] = jnp.exp(total - cum)
    for q in range(NX):
        tots[q] = jnp.broadcast_to(total[:, q * lanes : (q + 1) * lanes], (8, lanes))
    k_tx = new(NX)
    for d in range(1, NX):
        links.send(k_tx + d, tots.at[at_x(d)], tots_x.at[x], dev_x(d))
    tots_x[x] = tots[x]

    loads[3].wait()
    loads[4].wait()
    b_all, c_all = bv[...], cv[...]
    scores = dot_t(c_all, b_all, PRECISE)
    scores_t = dot_t(b_all, c_all, PRECISE)
    b_t[...] = b_all.T.astype(BF16)
    c_t[...] = c_all.T.astype(BF16)

    def span_weights(h):
        down = jnp.broadcast_to(cum[:, h * head_dim : h * head_dim + 1], (tok, tok))
        across = jnp.broadcast_to(cum_row[h : h + 1, :], (tok, tok))
        fall = jnp.exp(jnp.minimum(down - across, 0.0))
        wts[h] = (jnp.where(lower, fall, 0.0) * scores).astype(BF16)
        rise = jnp.exp(jnp.minimum(across - down, 0.0))
        wts_t[h] = (jnp.where(ones_s >= ones_t, rise, 0.0) * scores_t).astype(BF16)

    def project(blk, first=False):
        m = mix[blk]
        for i, w in enumerate((wx, wz)):
            span = slice(i * width, (i + 1) * width)
            term = dot(m, w[blk])
            acc[:, span] = term if first else acc[:, span] + term

    for h in range(0, 2):
        span_weights(h)
    loads[7].wait()
    loads[8].wait()
    project(head, True)

    links.arrive(k_r + LO, piece(blk_l, LO), left)
    links.send(k_fr, piece(blk_l, LO), piece(blk_l, LO), right)
    hand_on("l", blk_l, LO)
    links.arrive(k_l + HI, piece(blk_r, HI), right)
    links.send(k_fl, piece(blk_r, HI), piece(blk_r, HI), left)
    hand_on("r", blk_r, HI)

    for d in range(1, NX):
        links.arrive(k_tx + d, tots_x.at[at_x(NX - d)], dev_x(d))
    group[...] = tots_x[0] + tots_x[1] + tots_x[2] + tots_x[3]
    k_tz = new(nz)
    for d in range(1, nz):
        links.send(k_tz + d, group, groups.at[z], dev_z(d))

    links.arrive(k_own, mix.at[head + other], sib)
    project(head + other)
    for h in range(2, 4):
        span_weights(h)

    links.arrive(k_r + HI, piece(blk_l, HI), left)
    hand_on("l", blk_l, HI)
    links.arrive(k_l + LO, piece(blk_r, LO), right)
    hand_on("r", blk_r, LO)
    for h in range(4, heads):
        span_weights(h)

    loads[5].wait()
    loads[6].wait()
    classes = cwv.shape[1]
    is_label = lax.broadcasted_iota(jnp.int32, (128, tok), 0) == labv[...]
    onehot = jnp.where(is_label, 1.0, 0.0).astype(F32).T[:, :classes].astype(BF16)
    cols[...] = dot_t(onehot, cwv[...])
    for d in range(1, nz):
        links.arrive(k_tz + d, groups.at[at_z(nz - d)], dev_z(d))

    project(blk_l)
    project(blk_r)
    from_sib("l", blk_l + other)
    project(blk_l + other)
    from_sib("r", blk_r + other)
    project(blk_r + other)
    links.arrive(k_fr, piece(blk_o, LO), left)
    hand_on("o", blk_o, LO)
    links.arrive(k_fl, piece(blk_o, HI), right)
    hand_on("o", blk_o, HI)
    project(blk_o)
    from_sib("o", blk_o + other)
    project(blk_o + other)

    def quarter(q):
        return slice(q * lanes, (q + 1) * lanes)

    xs = acc[:, :width]
    x_end = dot(b_t[...], (xs * dec_out[...]).astype(BF16)).astype(BF16)
    for q in range(NX):
        f_send[q] = x_end[:, quarter(q)]
    k_ax = new(NX)
    for d in range(1, NX):
        links.send(k_ax + d, f_send.at[at_x(d)], f_x.at[x], dev_x(d))
    f_x[x] = f_send[x]

    zs = acc[:, width:]
    sig = jax.nn.sigmoid(zs)
    grad_y = cols[...] * (zs * sig)
    g_end = dot(c_t[...], (grad_y * dec_in[...]).astype(BF16)).astype(BF16)
    for q in range(NX):
        b_send[q] = g_end[:, quarter(q)]
    k_ab = new(NX)
    for d in range(1, NX):
        links.send(k_ab + d, b_send.at[at_x(d)], b_x.at[x], dev_x(d))
    b_x[x] = b_send[x]
    fz[...] = cols[...] * sig * (1.0 + zs * (1.0 - sig))

    def fall_of(i):
        return jnp.exp(tots_x[i, 0:1, :])

    for d in range(1, NX):
        links.arrive(k_ax + d, f_x.at[at_x(NX - d)], dev_x(d))
    run = jnp.zeros((state, lanes), F32)
    for i in range(NX):
        f_pre[i] = run
        run = fall_of(i) * run + f_x[i].astype(F32)
    f_tot[...] = run.astype(BF16)
    k_z = new(nz)

    def send_f(d, carry):
        links.make(k_z + d, f_tot, t_z.at[z], {"seq": (z + d) * NX + x}).start()
        return carry

    lax.fori_loop(1, nz - z, send_f, 0)

    for d in range(1, NX):
        links.arrive(k_ab + d, b_x.at[at_x(NX - d)], dev_x(d))
    run = jnp.zeros((state, lanes), F32)
    for i in reversed(range(NX)):
        b_pre[i] = run
        run = fall_of(i) * run + b_x[i].astype(F32)
    b_tot[...] = run.astype(BF16)

    def send_b(d, carry):
        links.make(k_z + d, b_tot, t_z.at[z], {"seq": (z + d - nz) * NX + x}).start()
        return carry

    lax.fori_loop(nz - z, nz, send_b, 0)

    lane = lax.broadcasted_iota(jnp.int32, (tok, lanes), 1)
    first_head = lane < head_dim
    one = lax.broadcasted_iota(jnp.int32, (1, lanes), 1)
    for q in range(NX):
        span = quarter(q)
        gain = jnp.where(one < head_dim, skip_s[2 * q], skip_s[2 * q + 1])
        xq = acc[:, span]
        xb = xq.astype(BF16)
        y_loc[:, span] = (
            jnp.where(first_head, dot(wts[2 * q], xb), dot(wts[2 * q + 1], xb)) + gain * xq
        )
        gq = grad_y[:, span]
        gb = gq.astype(BF16)
        gx_loc[:, span] = (
            jnp.where(first_head, dot(wts_t[2 * q], gb), dot(wts_t[2 * q + 1], gb)) + gain * gq
        )

    def join(i, carry):
        return jnp.exp(groups[i, 0:1, :]) * carry + t_z[i].astype(F32)

    def from_earlier(i, carry):
        links.arrive(k_z + z - i, t_z.at[i], dev_z(1))
        return join(i, carry)

    carry = lax.fori_loop(0, z, from_earlier, jnp.zeros((state, lanes), F32))
    fall = jnp.ones((1, lanes), F32)
    for i in range(NX):
        f_back[i] = (f_pre[i] + fall * carry).astype(BF16)
        fall = fall * fall_of(i)
    k_bf = new(NX)
    for d in range(1, NX):
        links.send(k_bf + d, f_back.at[at_x(d)], f_in.at[x], dev_x(d))
    f_in[x] = f_back[x]

    def from_later(i, carry):
        source = nz - 1 - i
        links.arrive(k_z + nz + z - source, t_z.at[source], dev_z(1))
        return join(source, carry)

    carry = lax.fori_loop(0, nz - 1 - z, from_later, jnp.zeros((state, lanes), F32))
    fall = jnp.ones((1, lanes), F32)
    for i in reversed(range(NX)):
        b_back[i] = (b_pre[i] + fall * carry).astype(BF16)
        fall = fall * fall_of(i)
    k_bb = new(NX)
    for d in range(1, NX):
        links.send(k_bb + d, b_back.at[at_x(d)], b_in.at[x], dev_x(d))
    b_in[x] = b_back[x]

    b_all, c_all = bv[...].astype(BF16), cv[...].astype(BF16)
    for d in range(1, NX):
        links.arrive(k_bf + d, f_in.at[at_x(NX - d)], dev_x(d))
    for q in range(NX):
        span = quarter(q)
        out_y = y_loc[:, span] + dec_in[:, span] * dot(c_all, f_in[q])
        gz[:, span] = (fz[:, span] * out_y).astype(BF16)
    for d in range(1, NX):
        links.arrive(k_bb + d, b_in.at[at_x(NX - d)], dev_x(d))
    for q in range(NX):
        span = quarter(q)
        gx[:, span] = (gx_loc[:, span] + dec_out[:, span] * dot(b_all, b_in[q])).astype(BF16)

    def share(blk):
        return dot_t(gx[...], wx[blk]) + dot_t(gz[...], wz[blk])

    k_rs = new(4)

    def to_sib(slot, blk):
        s_sib[slot] = share(blk + other).astype(BF16)
        links.send(k_rs + slot, s_sib.at[slot], r_sib.at[slot], sib)

    def both(slot, blk):
        mine = share(blk)
        links.arrive(k_rs + slot, r_sib.at[slot], sib)
        return mine + r_sib[slot].astype(F32)

    k_or, k_ol = new(), new()
    k_er, k_el = new(2), new(2)
    lo, hi = part
    to_sib(0, blk_o)
    to_sib(1, blk_r)
    cs_opp[...] = both(0, blk_o).astype(BF16)
    links.send(k_or, cs_opp.at[lo], r_lo, right)
    links.send(k_ol, cs_opp.at[hi], r_hi, left)
    to_sib(2, blk_l)
    cs_r[...] = both(1, blk_r)
    s_right[hi, :] = cs_r[hi, :].astype(BF16)
    links.send(k_er + HI, s_right.at[hi], r_left.at[hi], right)
    cs_l[...] = both(2, blk_l)
    s_left[lo, :] = cs_l[lo, :].astype(BF16)
    links.send(k_el + LO, s_left.at[lo], r_right.at[lo], left)
    to_sib(3, head)
    links.arrive(k_or, r_lo, left)
    s_right[lo, :] = (cs_r[lo, :] + r_lo[...].astype(F32)).astype(BF16)
    links.send(k_er + LO, s_right.at[lo], r_left.at[lo], right)
    links.arrive(k_ol, r_hi, right)
    s_left[hi, :] = (cs_l[hi, :] + r_hi[...].astype(F32)).astype(BF16)
    links.send(k_el + HI, s_left.at[hi], r_right.at[hi], left)
    outv[...] = both(3, head)

    def finish(rows, first, second, i):
        outv[rows, :] = outv[rows, :] + (r_left[rows, :].astype(F32) + r_right[rows, :].astype(F32))
        copy = pltpu.make_async_copy(outv.at[rows], out_h.at[rows], local_sems.at[len(pairs) + i])
        copy.start()
        return copy

    links.arrive(k_el + LO, r_right.at[lo], right)
    links.arrive(k_er + LO, r_left.at[lo], left)
    done_lo = finish(lo, 0, 0, 0)
    links.arrive(k_er + HI, r_left.at[hi], left)
    links.arrive(k_el + HI, r_right.at[hi], right)
    done_hi = finish(hi, 0, 0, 1)

    def sent_f(d, carry):
        links.make(k_z + d, f_tot, f_tot, dev_z(1)).wait_send()
        return carry

    lax.fori_loop(1, nz, sent_f, 0)
    links.finish()
    done_lo.wait()
    done_hi.wait()


SEMS = 96


def local(
    embedding,
    noise_draw,
    weight_x,
    weight_z,
    b_proj,
    c_proj,
    log_decay,
    skip_gain,
    class_weight,
    true_label,
):
    tok, feat = embedding.shape
    width = weight_x.shape[1]
    heads = skip_gain.shape[0]
    state = b_proj.shape[1]
    classes = class_weight.shape[1]
    n_head = lax.axis_size("head")
    nz = lax.axis_size("seq") // NX
    ny = n_head // 2
    lanes = width // NX
    half = tok // 2
    vm = pltpu.VMEM
    quarters = [vm((NX, state, lanes), BF16)] * 2
    scratch = [
        vm((tok, feat), BF16),
        vm((tok, feat), BF16),
        vm((n_head, feat, width), BF16),
        vm((n_head, feat, width), BF16),
        vm((tok, state), F32),
        vm((tok, state), F32),
        vm((heads, tok), F32),
        vm((width, classes), BF16),
        vm((1, tok), jnp.int32),
        vm((n_head, tok, feat), BF16),
        vm((tok, 2 * width), F32),
        vm((tok, width), F32),
        vm((tok, width), F32),
        vm((tok, width), F32),
        vm((heads, tok, tok), BF16),
        vm((heads, tok, tok), BF16),
        vm((state, tok), BF16),
        vm((state, tok), BF16),
        vm((NX, 8, lanes), F32),
        vm((NX, 8, lanes), F32),
        vm((8, lanes), F32),
        vm((nz, 8, lanes), F32),
        *quarters,
        *quarters,
        vm((NX, state, lanes), F32),
        vm((NX, state, lanes), F32),
        vm((state, lanes), BF16),
        vm((state, lanes), BF16),
        vm((nz, state, lanes), BF16),
        *quarters,
        *quarters,
        vm((tok, width), F32),
        vm((tok, width), F32),
        vm((tok, width), F32),
        vm((tok, width), BF16),
        vm((tok, width), BF16),
        vm((4, tok, feat), BF16),
        vm((4, tok, feat), BF16),
        vm((tok, feat), BF16),
        vm((half, feat), BF16),
        vm((half, feat), BF16),
        vm((tok, feat), F32),
        vm((tok, feat), F32),
        vm((tok, feat), BF16),
        vm((tok, feat), BF16),
        vm((tok, feat), BF16),
        vm((tok, feat), BF16),
        vm((tok, feat), F32),
        pltpu.SemaphoreType.DMA((11,)),
        pltpu.SemaphoreType.DMA((SEMS,)),
        pltpu.SemaphoreType.DMA((SEMS,)),
    ]
    anywhere = pl.BlockSpec(memory_space=pl.ANY)
    return pl.pallas_call(
        functools.partial(kernel, nz, ny),
        out_shape=jax.ShapeDtypeStruct((tok, feat), F32),
        in_specs=[anywhere] * 9 + [pl.BlockSpec(memory_space=pltpu.SMEM)],
        out_specs=anywhere,
        scratch_shapes=scratch,
        compiler_params=pltpu.CompilerParams(
            collective_id=0, has_side_effects=True, vmem_limit_bytes=60 * 1024 * 1024
        ),
        cost_estimate=pl.CostEstimate(
            flops=8 * tok * feat * n_head * width,
            bytes_accessed=10 * 1024 * 1024,
            transcendentals=heads * tok * tok * 2,
        ),
    )(
        embedding,
        noise_draw,
        weight_x.reshape(n_head, feat, width),
        weight_z.reshape(n_head, feat, width),
        b_proj,
        c_proj,
        log_decay,
        class_weight,
        true_label.reshape(1, tok),
        skip_gain,
    )


def solution(mesh):
    return jax.shard_map(
        local,
        mesh=mesh,
        in_specs=(
            P("seq", "head"),
            P("seq", "head"),
            P(None, "head"),
            P(None, "head"),
            P("seq", None),
            P("seq", None),
            P("head", "seq"),
            P("head"),
            P("head", None),
            P("seq"),
        ),
        out_specs=P("seq", "head"),
        check_vma=False,
    )
```

```python
import functools

import jax
import jax.numpy as jnp
from jax import lax
from jax.experimental import pallas as pl
from jax.experimental.pallas import tpu as pltpu
from jax.sharding import PartitionSpec as P

F32 = jnp.float32
BF16 = jnp.bfloat16
MESH = pl.DeviceIdType.MESH
NX = 4
NP = 2
NG = NP * NX
PRECISE = lax.Precision.HIGHEST
LO, HI = 0, 1


def dot(a, b):
    return jnp.dot(a, b, preferred_element_type=F32)


def dot_t(a, b, precision=None):
    return lax.dot_general(
        a, b, (((1,), (1,)), ((), ())), preferred_element_type=F32, precision=precision
    )


class Links:
    def __init__(self, send_sems, recv_sems):
        self.send_sems, self.recv_sems = send_sems, recv_sems
        self.sent = []

    def make(self, k, src, dst, device):
        return pltpu.make_async_remote_copy(
            src_ref=src,
            dst_ref=dst,
            send_sem=self.send_sems.at[k],
            recv_sem=self.recv_sems.at[k],
            device_id=device,
            device_id_type=MESH,
        )

    def send(self, k, src, dst, device):
        copy = self.make(k, src, dst, device)
        copy.start()
        self.sent.append(copy)

    def arrive(self, k, dst, device):
        self.make(k, dst, dst, device).wait_recv()

    def finish(self):
        for copy in self.sent:
            copy.wait_send()


def kernel(
    nz,
    ny,
    emb_h,
    noise_h,
    wx_h,
    wz_h,
    b_h,
    c_h,
    ld_h,
    cw_h,
    lab_h,
    skip_s,
    out,
    ev,
    nv,
    wx,
    wz,
    bv,
    cv,
    ldv,
    cwv,
    labv,
    mix,
    acc,
    dec_in,
    dec_out,
    cols,
    wts,
    wts_t,
    b_t,
    c_t,
    tots,
    tots_m,
    group,
    groups,
    f_send,
    b_send,
    f_x,
    b_x,
    f_pre,
    b_pre,
    f_tot,
    b_tot,
    t_g,
    f_back,
    b_back,
    f_in,
    b_in,
    y_loc,
    gx_loc,
    fz,
    gx,
    gz,
    s_sib,
    r_sib,
    cs_opp,
    r_lo,
    r_hi,
    cs_r,
    cs_l,
    s_right,
    s_left,
    r_left,
    r_right,
    outv,
    early,
    local_sems,
    send_sems,
    recv_sems,
):
    tok, feat = ev.shape
    half = tok // 2
    width = acc.shape[1] // 2
    heads = ldv.shape[0]
    head_dim = width // heads
    state = bv.shape[1]
    lanes = width // NX
    seq, head = lax.axis_index("seq"), lax.axis_index("head")
    z, x = seq // NX, seq % NX
    y, core = head // 2, head % 2
    other = 1 - 2 * core

    links = Links(send_sems, recv_sems)
    counter = [0]

    def new(count=1):
        first = counter[0]
        counter[0] += count
        return first

    pairs = [
        (emb_h, ev),
        (noise_h, nv),
        (ld_h, ldv),
        (b_h, bv),
        (c_h, cv),
        (cw_h, cwv),
        (lab_h, labv),
        (wx_h, wx),
        (wz_h, wz),
    ]
    loads = [pltpu.make_async_copy(s, d, local_sems.at[i]) for i, (s, d) in enumerate(pairs)]
    for load in loads:
        load.start()

    sib = {"head": head + other}
    blk_r = ((y + 1) % ny) * 2 + core
    blk_l = ((y + ny - 1) % ny) * 2 + core
    blk_o = ((y + 2) % ny) * 2 + core
    right, left = {"head": blk_r}, {"head": blk_l}

    ng = nz // NP
    me, mine = (z % NP) * NX + x, z // NP

    def at_m(d):
        return (me + d) % NG

    def at_g(d):
        return (mine + d) % ng

    def dev_m(d):
        return {"seq": mine * NG + at_m(d)}

    def dev_g(d):
        return {"seq": at_g(d) * NG + me}

    barrier = pltpu.get_barrier_semaphore()
    partners = [sib, right, left]
    partners += [dev_m(d) for d in range(1, NG)] + [dev_g(d) for d in range(1, ng)]
    for partner in partners:
        pl.semaphore_signal(barrier, inc=1, device_id=partner, device_id_type=MESH)

    loads[0].wait()
    loads[1].wait()
    mix[head] = (ev[...].astype(F32) + nv[...].astype(F32)).astype(BF16)
    pl.semaphore_wait(barrier, len(partners))

    part = (pl.ds(0, half), pl.ds(half, half))

    def piece(blk, h):
        return mix.at[blk, part[h]]

    k_r, k_l, k_own = new(2), new(2), new()
    k_fr, k_fl = new(), new()
    k_sib = {name: new(2) for name in ("l", "r", "o")}

    def hand_on(name, blk, h):
        links.send(k_sib[name] + h, piece(blk, h), piece(blk, h), sib)

    def from_sib(name, blk):
        for h in (LO, HI):
            links.arrive(k_sib[name] + h, piece(blk, h), sib)

    links.send(k_r + LO, piece(head, LO), piece(head, LO), right)
    links.send(k_l + HI, piece(head, HI), piece(head, HI), left)
    links.send(k_own, mix.at[head], mix.at[head], sib)
    links.send(k_r + HI, piece(head, HI), piece(head, HI), right)
    links.send(k_l + LO, piece(head, LO), piece(head, LO), left)

    loads[2].wait()
    rates = ldv[...]
    ones_t = lax.broadcasted_iota(jnp.int32, (tok, tok), 0)
    ones_s = lax.broadcasted_iota(jnp.int32, (tok, tok), 1)
    lower = ones_t >= ones_s
    tri = jnp.where(lower, 1.0, 0.0).astype(F32)
    tri_t = jnp.where(ones_s >= ones_t, 1.0, 0.0).astype(F32)
    cum_row = jnp.dot(rates, tri_t, preferred_element_type=F32, precision=PRECISE)
    wide = jnp.concatenate(
        [jnp.broadcast_to(rates[h : h + 1, :], (head_dim, tok)) for h in range(heads)], axis=0
    )
    cum = dot_t(tri, wide, PRECISE)
    total = cum[tok - 1 : tok, :]
    dec_in[...] = jnp.exp(cum)
    dec_out[...] = jnp.exp(total - cum)
    for q in range(NX):
        tots[q] = jnp.broadcast_to(total[:, q * lanes : (q + 1) * lanes], (8, lanes))
    k_tm = new(NG)
    for d in range(1, NG):
        links.send(k_tm + d, tots.at[at_m(d) % NX], tots_m.at[me], dev_m(d))
    tots_m[me] = tots[x]

    links.arrive(k_r + LO, piece(blk_l, LO), left)
    links.send(k_fr, piece(blk_l, LO), piece(blk_l, LO), right)
    hand_on("l", blk_l, LO)
    links.arrive(k_l + HI, piece(blk_r, HI), right)
    links.send(k_fl, piece(blk_r, HI), piece(blk_r, HI), left)
    hand_on("r", blk_r, HI)

    loads[5].wait()
    loads[6].wait()
    classes = cwv.shape[0]
    is_label = lax.broadcasted_iota(jnp.int32, (128, tok), 0) == labv[...]
    onehot = jnp.where(is_label, 1.0, 0.0).astype(F32).T[:, :classes].astype(BF16)
    cols[...] = dot(onehot, cwv[...])

    loads[3].wait()
    loads[4].wait()
    b_all, c_all = bv[...], cv[...]
    scores = dot_t(c_all, b_all, PRECISE)
    scores_t = dot_t(b_all, c_all, PRECISE)
    b_t[...] = b_all.T.astype(BF16)
    c_t[...] = c_all.T.astype(BF16)

    def span_weights(h):
        down = jnp.broadcast_to(cum[:, h * head_dim : h * head_dim + 1], (tok, tok))
        across = jnp.broadcast_to(cum_row[h : h + 1, :], (tok, tok))
        fall = jnp.exp(jnp.minimum(down - across, 0.0))
        wts[h] = (jnp.where(lower, fall, 0.0) * scores).astype(BF16)
        rise = jnp.exp(jnp.minimum(across - down, 0.0))
        wts_t[h] = (jnp.where(ones_s >= ones_t, rise, 0.0) * scores_t).astype(BF16)

    def project(blk, first=False):
        m = mix[blk]
        for i, w in enumerate((wx, wz)):
            span = slice(i * width, (i + 1) * width)
            term = dot(m, w[blk])
            acc[:, span] = term if first else acc[:, span] + term

    for h in range(0, 2):
        span_weights(h)
    loads[7].wait()
    loads[8].wait()
    project(head, True)

    links.arrive(k_own, mix.at[head + other], sib)
    links.arrive(k_r + HI, piece(blk_l, HI), left)
    hand_on("l", blk_l, HI)
    links.arrive(k_l + LO, piece(blk_r, LO), right)
    hand_on("r", blk_r, LO)
    project(head + other)

    for d in range(1, NG):
        links.arrive(k_tm + d, tots_m.at[at_m(NG - d)], dev_m(d))
    group[...] = functools.reduce(lambda a, b: a + b, [tots_m[i] for i in range(NG)])
    k_tg = new(ng)
    for d in range(1, ng):
        links.send(k_tg + d, group, groups.at[mine], dev_g(d))

    project(blk_l)
    project(blk_r)
    from_sib("l", blk_l + other)
    project(blk_l + other)
    from_sib("r", blk_r + other)
    project(blk_r + other)
    for h in range(2, 4):
        span_weights(h)

    links.arrive(k_fr, piece(blk_o, LO), left)
    hand_on("o", blk_o, LO)
    links.arrive(k_fl, piece(blk_o, HI), right)
    hand_on("o", blk_o, HI)
    project(blk_o)
    from_sib("o", blk_o + other)
    project(blk_o + other)

    def quarter(q):
        return slice(q * lanes, (q + 1) * lanes)

    xs = acc[:, :width]
    x_end = dot(b_t[...], (xs * dec_out[...]).astype(BF16)).astype(BF16)
    rows = state // NP
    for i in range(NG):
        f_send[i] = x_end[i // NX * rows : (i // NX + 1) * rows, quarter(i % NX)]
    k_ax = new(NG)
    for d in range(1, NG):
        links.send(k_ax + d, f_send.at[at_m(d)], f_x.at[me], dev_m(d))
    f_x[me] = f_send[me]

    zs = acc[:, width:]
    sig = jax.nn.sigmoid(zs)
    grad_y = cols[...] * (zs * sig)
    g_end = dot(c_t[...], (grad_y * dec_in[...]).astype(BF16)).astype(BF16)
    for i in range(NG):
        b_send[i] = g_end[i // NX * rows : (i // NX + 1) * rows, quarter(i % NX)]
    k_ab = new(NG)
    for d in range(1, NG):
        links.send(k_ab + d, b_send.at[at_m(d)], b_x.at[me], dev_m(d))
    b_x[me] = b_send[me]
    fz[...] = cols[...] * sig * (1.0 + zs * (1.0 - sig))
    for h in range(4, heads):
        span_weights(h)
    for d in range(1, ng):
        links.arrive(k_tg + d, groups.at[at_g(ng - d)], dev_g(d))

    def fall_of(i):
        return jnp.exp(tots_m[i, 0:1, :])

    def nothing():
        return jnp.zeros((rows, lanes), F32)

    for d in range(1, NG):
        links.arrive(k_ax + d, f_x.at[at_m(NG - d)], dev_m(d))
    run = nothing()
    for i in range(NG):
        f_pre[i] = run
        run = fall_of(i) * run + f_x[i].astype(F32)
    f_tot[...] = run.astype(BF16)
    k_g = new(ng)

    def send_f(d, carry):
        links.make(k_g + d, f_tot, t_g.at[mine], {"seq": (mine + d) * NG + me}).start()
        return carry

    lax.fori_loop(1, ng - mine, send_f, 0)

    for d in range(1, NG):
        links.arrive(k_ab + d, b_x.at[at_m(NG - d)], dev_m(d))
    run = nothing()
    for i in reversed(range(NG)):
        b_pre[i] = run
        run = fall_of(i) * run + b_x[i].astype(F32)
    b_tot[...] = run.astype(BF16)

    def send_b(d, carry):
        links.make(k_g + d, b_tot, t_g.at[mine], {"seq": (mine + d - ng) * NG + me}).start()
        return carry

    lax.fori_loop(ng - mine, ng, send_b, 0)

    lane = lax.broadcasted_iota(jnp.int32, (tok, lanes), 1)
    first_head = lane < head_dim
    one = lax.broadcasted_iota(jnp.int32, (1, lanes), 1)
    for q in range(NX):
        span = quarter(q)
        gain = jnp.where(one < head_dim, skip_s[2 * q], skip_s[2 * q + 1])
        xq = acc[:, span]
        xb = xq.astype(BF16)
        y_loc[:, span] = (
            jnp.where(first_head, dot(wts[2 * q], xb), dot(wts[2 * q + 1], xb)) + gain * xq
        )
        gq = grad_y[:, span]
        gb = gq.astype(BF16)
        gx_loc[:, span] = (
            jnp.where(first_head, dot(wts_t[2 * q], gb), dot(wts_t[2 * q + 1], gb)) + gain * gq
        )

    def join(i, carry):
        return jnp.exp(groups[i, 0:1, :]) * carry + t_g[i].astype(F32)

    def from_earlier(i, carry):
        links.arrive(k_g + mine - i, t_g.at[i], dev_g(1))
        return join(i, carry)

    carry = lax.fori_loop(0, mine, from_earlier, nothing())
    fall = jnp.ones((1, lanes), F32)
    for i in range(NG):
        f_back[i] = (f_pre[i] + fall * carry).astype(BF16)
        fall = fall * fall_of(i)
    k_bf = new(NG)
    for d in range(1, NG):
        links.send(k_bf + d, f_back.at[at_m(d)], f_in.at[me], dev_m(d))
    f_in[me] = f_back[me]

    def from_later(i, carry):
        source = ng - 1 - i
        links.arrive(k_g + ng + mine - source, t_g.at[source], dev_g(1))
        return join(source, carry)

    carry = lax.fori_loop(0, ng - 1 - mine, from_later, nothing())
    fall = jnp.ones((1, lanes), F32)
    for i in reversed(range(NG)):
        b_back[i] = (b_pre[i] + fall * carry).astype(BF16)
        fall = fall * fall_of(i)
    k_bb = new(NG)
    for d in range(1, NG):
        links.send(k_bb + d, b_back.at[at_m(d)], b_in.at[me], dev_m(d))
    b_in[me] = b_back[me]

    def whole(pieces, q):
        return jnp.concatenate([pieces[q + p * NX] for p in range(NP)], axis=0)

    b_all, c_all = bv[...].astype(BF16), cv[...].astype(BF16)
    for d in range(1, NG):
        links.arrive(k_bf + d, f_in.at[at_m(NG - d)], dev_m(d))
    for q in range(NX):
        span = quarter(q)
        out_y = y_loc[:, span] + dec_in[:, span] * dot(c_all, whole(f_in, q))
        gz[:, span] = (fz[:, span] * out_y).astype(BF16)
    for i, blk in enumerate((blk_o + other, blk_o)):
        early[i] = dot_t(gz[...], wz[blk])
    for d in range(1, NG):
        links.arrive(k_bb + d, b_in.at[at_m(NG - d)], dev_m(d))
    for q in range(NX):
        span = quarter(q)
        gx[:, span] = (gx_loc[:, span] + dec_out[:, span] * dot(b_all, whole(b_in, q))).astype(BF16)

    def share(blk, done=None):
        from_z = dot_t(gz[...], wz[blk]) if done is None else early[done]
        return dot_t(gx[...], wx[blk]) + from_z

    k_rs = new(4)

    def to_sib(slot, blk, done=None):
        s_sib[slot] = share(blk + other, done).astype(BF16)
        links.send(k_rs + slot, s_sib.at[slot], r_sib.at[slot], sib)

    def both(slot, blk, done=None):
        own = share(blk, done)
        links.arrive(k_rs + slot, r_sib.at[slot], sib)
        return own + r_sib[slot].astype(F32)

    k_or, k_ol = new(), new()
    k_er, k_el = new(2), new(2)
    lo, hi = part
    to_sib(0, blk_o, 0)
    to_sib(1, blk_r)
    cs_opp[...] = both(0, blk_o, 1).astype(BF16)
    links.send(k_or, cs_opp.at[lo], r_lo, right)
    links.send(k_ol, cs_opp.at[hi], r_hi, left)
    to_sib(2, blk_l)
    cs_r[...] = both(1, blk_r)
    s_right[hi, :] = cs_r[hi, :].astype(BF16)
    links.send(k_er + HI, s_right.at[hi], r_left.at[hi], right)
    cs_l[...] = both(2, blk_l)
    s_left[lo, :] = cs_l[lo, :].astype(BF16)
    links.send(k_el + LO, s_left.at[lo], r_right.at[lo], left)
    to_sib(3, head)
    links.arrive(k_or, r_lo, left)
    s_right[lo, :] = (cs_r[lo, :] + r_lo[...].astype(F32)).astype(BF16)
    links.send(k_er + LO, s_right.at[lo], r_left.at[lo], right)
    links.arrive(k_ol, r_hi, right)
    s_left[hi, :] = (cs_l[hi, :] + r_hi[...].astype(F32)).astype(BF16)
    links.send(k_el + HI, s_left.at[hi], r_right.at[hi], left)
    outv[...] = both(3, head)

    def finish(rows):
        out[rows, :] = outv[rows, :] + (r_left[rows, :].astype(F32) + r_right[rows, :].astype(F32))

    links.arrive(k_el + LO, r_right.at[lo], right)
    links.arrive(k_er + LO, r_left.at[lo], left)
    finish(lo)
    links.arrive(k_er + HI, r_left.at[hi], left)
    links.arrive(k_el + HI, r_right.at[hi], right)
    finish(hi)

    def sent_f(d, carry):
        links.make(k_g + d, f_tot, f_tot, dev_g(1)).wait_send()
        return carry

    lax.fori_loop(1, ng, sent_f, 0)
    links.finish()


SEMS = 96


def local(
    embedding,
    noise_draw,
    weight_x,
    weight_z,
    b_proj,
    c_proj,
    log_decay,
    skip_gain,
    class_weight,
    true_label,
):
    tok, feat = embedding.shape
    width = weight_x.shape[1]
    heads = skip_gain.shape[0]
    state = b_proj.shape[1]
    classes = class_weight.shape[1]
    n_head = lax.axis_size("head")
    nz = lax.axis_size("seq") // NX
    ny = n_head // 2
    lanes = width // NX
    half = tok // 2
    vm = pltpu.VMEM
    rows = state // NP
    eighths = [vm((NG, rows, lanes), BF16)] * 2
    scratch = [
        vm((tok, feat), BF16),
        vm((tok, feat), BF16),
        vm((n_head, feat, width), BF16),
        vm((n_head, feat, width), BF16),
        vm((tok, state), F32),
        vm((tok, state), F32),
        vm((heads, tok), F32),
        vm((classes, width), BF16),
        vm((1, tok), jnp.int32),
        vm((n_head, tok, feat), BF16),
        vm((tok, 2 * width), F32),
        vm((tok, width), F32),
        vm((tok, width), F32),
        vm((tok, width), F32),
        vm((heads, tok, tok), BF16),
        vm((heads, tok, tok), BF16),
        vm((state, tok), BF16),
        vm((state, tok), BF16),
        vm((NX, 8, lanes), F32),
        vm((NG, 8, lanes), F32),
        vm((8, lanes), F32),
        vm((nz // NP, 8, lanes), F32),
        *eighths,
        *eighths,
        vm((NG, rows, lanes), F32),
        vm((NG, rows, lanes), F32),
        vm((rows, lanes), BF16),
        vm((rows, lanes), BF16),
        vm((nz // NP, rows, lanes), BF16),
        *eighths,
        *eighths,
        vm((tok, width), F32),
        vm((tok, width), F32),
        vm((tok, width), F32),
        vm((tok, width), BF16),
        vm((tok, width), BF16),
        vm((4, tok, feat), BF16),
        vm((4, tok, feat), BF16),
        vm((tok, feat), BF16),
        vm((half, feat), BF16),
        vm((half, feat), BF16),
        vm((tok, feat), F32),
        vm((tok, feat), F32),
        vm((tok, feat), BF16),
        vm((tok, feat), BF16),
        vm((tok, feat), BF16),
        vm((tok, feat), BF16),
        vm((tok, feat), F32),
        vm((2, tok, feat), F32),
        pltpu.SemaphoreType.DMA((9,)),
        pltpu.SemaphoreType.DMA((SEMS,)),
        pltpu.SemaphoreType.DMA((SEMS,)),
    ]
    anywhere = pl.BlockSpec(memory_space=pl.ANY)
    return pl.pallas_call(
        functools.partial(kernel, nz, ny),
        out_shape=pltpu.VMEM((tok, feat), F32),
        in_specs=[anywhere] * 9 + [pl.BlockSpec(memory_space=pltpu.SMEM)],
        out_specs=pl.BlockSpec(memory_space=pltpu.VMEM),
        scratch_shapes=scratch,
        compiler_params=pltpu.CompilerParams(
            collective_id=0, has_side_effects=True, vmem_limit_bytes=60 * 1024 * 1024
        ),
        cost_estimate=pl.CostEstimate(
            flops=8 * tok * feat * n_head * width,
            bytes_accessed=10 * 1024 * 1024,
            transcendentals=heads * tok * tok * 2,
        ),
    )(
        embedding,
        noise_draw,
        weight_x.reshape(n_head, feat, width),
        weight_z.reshape(n_head, feat, width),
        b_proj,
        c_proj,
        log_decay,
        class_weight.T,
        true_label.reshape(1, tok),
        skip_gain,
    )


def solution(mesh):
    return jax.shard_map(
        local,
        mesh=mesh,
        in_specs=(
            P("seq", "head"),
            P("seq", "head"),
            P(None, "head"),
            P(None, "head"),
            P("seq", None),
            P("seq", None),
            P("head", "seq"),
            P("head"),
            P("head", None),
            P("seq"),
        ),
        out_specs=P("seq", "head"),
        check_vma=False,
    )
```

```python
import functools

import jax
import jax.numpy as jnp
from jax import lax
from jax.experimental import pallas as pl
from jax.experimental.pallas import tpu as pltpu
from jax.sharding import PartitionSpec as P

F32 = jnp.float32
BF16 = jnp.bfloat16
MESH = pl.DeviceIdType.MESH
NX = 4
NP = 2
NG = NP * NX
PRECISE = lax.Precision.HIGHEST
LO, HI = 0, 1
HALVES = (LO, HI)


def dot(a, b):
    return jnp.dot(a, b, preferred_element_type=F32)


def dot_t(a, b, precision=None):
    return lax.dot_general(
        a, b, (((1,), (1,)), ((), ())), preferred_element_type=F32, precision=precision
    )


class Links:
    def __init__(self, send_sems, recv_sems):
        self.send_sems, self.recv_sems = send_sems, recv_sems
        self.sent = []

    def make(self, k, src, dst, device):
        return pltpu.make_async_remote_copy(
            src_ref=src,
            dst_ref=dst,
            send_sem=self.send_sems.at[k],
            recv_sem=self.recv_sems.at[k],
            device_id=device,
            device_id_type=MESH,
        )

    def send(self, k, src, dst, device):
        copy = self.make(k, src, dst, device)
        copy.start()
        self.sent.append(copy)

    def arrive(self, k, dst, device):
        self.make(k, dst, dst, device).wait_recv()

    def finish(self):
        for copy in self.sent:
            copy.wait_send()


def kernel(
    nz,
    ny,
    emb_h,
    noise_h,
    wx_h,
    wz_h,
    b_h,
    c_h,
    ld_h,
    cw_h,
    lab_h,
    skip_s,
    out,
    ev,
    nv,
    wx,
    wz,
    bv,
    cv,
    ldv,
    cwv,
    labv,
    mix,
    acc,
    dec_in,
    dec_out,
    cols,
    wts,
    wts_t,
    b_t,
    c_t,
    tots,
    tots_m,
    group,
    groups,
    f_send,
    b_send,
    f_x,
    b_x,
    f_pre,
    b_pre,
    f_tot,
    b_tot,
    t_g,
    f_back,
    b_back,
    f_in,
    b_in,
    y_loc,
    gx_loc,
    fz,
    gx,
    gz,
    s_sib,
    r_sib,
    cs_opp,
    r_opp,
    cs_r,
    cs_l,
    s_right,
    s_left,
    r_left,
    r_right,
    outv,
    early,
    local_sems,
    relay,
    send_sems,
    recv_sems,
):
    tok, feat = ev.shape
    half = feat // 2
    width = acc.shape[1] // 2
    heads = ldv.shape[0]
    head_dim = width // heads
    state = bv.shape[1]
    lanes = width // NX
    seq, head = lax.axis_index("seq"), lax.axis_index("head")
    z, x = seq // NX, seq % NX
    y, core = head // 2, head % 2
    other = 1 - 2 * core

    links = Links(send_sems, recv_sems)
    counter = [0]

    def new(count=1):
        first = counter[0]
        counter[0] += count
        return first

    pairs = [
        (emb_h, ev),
        (noise_h, nv),
        (ld_h, ldv),
        (b_h, bv),
        (c_h, cv),
        (cw_h, cwv),
        (lab_h, labv),
        (wx_h, wx),
        (wz_h, wz),
    ]
    loads = [pltpu.make_async_copy(s, d, local_sems.at[i]) for i, (s, d) in enumerate(pairs)]
    for load in loads:
        load.start()

    sib = {"head": head + other}
    blk_r = ((y + 1) % ny) * 2 + core
    blk_l = ((y + ny - 1) % ny) * 2 + core
    blk_o = ((y + 2) % ny) * 2 + core
    right, left = {"head": blk_r}, {"head": blk_l}

    ng = nz // NP
    me, mine = (z % NP) * NX + x, z // NP

    def at_m(d):
        return (me + d) % NG

    def at_g(d):
        return (mine + d) % ng

    def dev_m(d):
        return {"seq": mine * NG + at_m(d)}

    def dev_g(d):
        return {"seq": at_g(d) * NG + me}

    barrier = pltpu.get_barrier_semaphore()
    near = [{"seq": z * NX + (x + d) % NX} for d in (1, NX - 1)]
    near += [{"seq": (z + d) % nz * NX + x} for d in (1, nz - 1)]
    partners = [sib, right, left] + near
    for partner in partners:
        pl.semaphore_signal(barrier, inc=1, device_id=partner, device_id_type=MESH)

    def tell(r):
        for partner in near:
            pl.semaphore_signal(relay.at[r], inc=1, device_id=partner, device_id_type=MESH)

    def told(r):
        pl.semaphore_wait(relay.at[r], len(near))

    loads[0].wait()
    loads[1].wait()
    noisy = (ev[...].astype(F32) + nv[...].astype(F32)).astype(BF16)
    for h in HALVES:
        mix[head, h] = noisy[:, h * half : (h + 1) * half]
    pl.semaphore_wait(barrier, len(partners))

    def piece(blk, h):
        return mix.at[blk, h]

    k_r, k_l, k_own = new(2), new(2), new()
    k_fr, k_fl = new(), new()
    k_sib = {name: new(2) for name in ("l", "r", "o")}

    def hand_on(name, blk, h):
        links.send(k_sib[name] + h, piece(blk, h), piece(blk, h), sib)

    def from_sib(name, blk, h):
        links.arrive(k_sib[name] + h, piece(blk, h), sib)

    links.send(k_r + LO, piece(head, LO), piece(head, LO), right)
    links.send(k_l + HI, piece(head, HI), piece(head, HI), left)
    links.send(k_own, mix.at[head], mix.at[head], sib)
    links.send(k_r + HI, piece(head, HI), piece(head, HI), right)
    links.send(k_l + LO, piece(head, LO), piece(head, LO), left)
    tell(0)

    loads[2].wait()
    rates = ldv[...]
    ones_t = lax.broadcasted_iota(jnp.int32, (tok, tok), 0)
    ones_s = lax.broadcasted_iota(jnp.int32, (tok, tok), 1)
    lower = ones_t >= ones_s
    tri = jnp.where(lower, 1.0, 0.0).astype(F32)
    tri_t = jnp.where(ones_s >= ones_t, 1.0, 0.0).astype(F32)
    cum_row = jnp.dot(rates, tri_t, preferred_element_type=F32, precision=PRECISE)
    wide = jnp.concatenate(
        [jnp.broadcast_to(rates[h : h + 1, :], (head_dim, tok)) for h in range(heads)], axis=0
    )
    cum = dot_t(tri, wide, PRECISE)
    total = cum[tok - 1 : tok, :]
    dec_in[...] = jnp.exp(cum)
    dec_out[...] = jnp.exp(total - cum)
    for q in range(NX):
        tots[q] = jnp.broadcast_to(total[:, q * lanes : (q + 1) * lanes], (8, lanes))
    tots_m[me] = tots[x]
    told(0)
    tell(1)

    links.arrive(k_r + LO, piece(blk_l, LO), left)
    links.send(k_fr, piece(blk_l, LO), piece(blk_l, LO), right)
    hand_on("l", blk_l, LO)
    links.arrive(k_l + HI, piece(blk_r, HI), right)
    links.send(k_fl, piece(blk_r, HI), piece(blk_r, HI), left)
    hand_on("r", blk_r, HI)
    told(1)
    tell(2)
    k_tm = new(NG)
    for d in range(1, NG):
        links.send(k_tm + d, tots.at[at_m(d) % NX], tots_m.at[me], dev_m(d))

    loads[5].wait()
    loads[6].wait()
    classes = cwv.shape[0]
    is_label = lax.broadcasted_iota(jnp.int32, (128, tok), 0) == labv[...]
    onehot = jnp.where(is_label, 1.0, 0.0).astype(F32).T[:, :classes].astype(BF16)
    cols[...] = dot(onehot, cwv[...])

    loads[3].wait()
    loads[4].wait()
    b_all, c_all = bv[...], cv[...]
    scores = dot_t(c_all, b_all, PRECISE)
    scores_t = dot_t(b_all, c_all, PRECISE)
    b_t[...] = b_all.T.astype(BF16)
    c_t[...] = c_all.T.astype(BF16)

    def span_weights(h):
        down = jnp.broadcast_to(cum[:, h * head_dim : h * head_dim + 1], (tok, tok))
        across = jnp.broadcast_to(cum_row[h : h + 1, :], (tok, tok))
        fall = jnp.exp(jnp.minimum(down - across, 0.0))
        wts[h] = (jnp.where(lower, fall, 0.0) * scores).astype(BF16)
        rise = jnp.exp(jnp.minimum(across - down, 0.0))
        wts_t[h] = (jnp.where(ones_s >= ones_t, rise, 0.0) * scores_t).astype(BF16)

    def project(blk, h, first=False):
        m = mix[blk, h]
        for i, w in enumerate((wx, wz)):
            span = slice(i * width, (i + 1) * width)
            term = dot(m, w[blk, h * half : (h + 1) * half, :])
            acc[:, span] = term if first else acc[:, span] + term

    for h in range(0, 2):
        span_weights(h)
    loads[7].wait()
    loads[8].wait()
    project(head, LO, True)
    project(head, HI)

    links.arrive(k_own, mix.at[head + other], sib)
    links.arrive(k_r + HI, piece(blk_l, HI), left)
    hand_on("l", blk_l, HI)
    links.arrive(k_l + LO, piece(blk_r, LO), right)
    hand_on("r", blk_r, LO)
    for h in HALVES:
        project(head + other, h)

    for d in range(1, NG):
        links.arrive(k_tm + d, tots_m.at[at_m(NG - d)], dev_m(d))
    group[...] = functools.reduce(lambda a, b: a + b, [tots_m[i] for i in range(NG)])
    told(2)
    k_tg = new(ng)
    for d in range(1, ng):
        links.send(k_tg + d, group, groups.at[mine], dev_g(d))

    for h in HALVES:
        project(blk_l, h)
        project(blk_r, h)
    for h in HALVES:
        from_sib("l", blk_l + other, h)
        project(blk_l + other, h)
        from_sib("r", blk_r + other, h)
        project(blk_r + other, h)

    links.arrive(k_fr, piece(blk_o, LO), left)
    hand_on("o", blk_o, LO)
    links.arrive(k_fl, piece(blk_o, HI), right)
    hand_on("o", blk_o, HI)
    for h in HALVES:
        project(blk_o, h)
    for h in HALVES:
        from_sib("o", blk_o + other, h)
        project(blk_o + other, h)

    def quarter(q):
        return slice(q * lanes, (q + 1) * lanes)

    xs = acc[:, :width]
    x_end = dot(b_t[...], (xs * dec_out[...]).astype(BF16)).astype(BF16)
    rows = state // NP
    for i in range(NG):
        f_send[i] = x_end[i // NX * rows : (i // NX + 1) * rows, quarter(i % NX)]
    k_ax = new(NG)
    for d in range(1, NG):
        links.send(k_ax + d, f_send.at[at_m(d)], f_x.at[me], dev_m(d))
    f_x[me] = f_send[me]

    zs = acc[:, width:]
    sig = jax.nn.sigmoid(zs)
    grad_y = cols[...] * (zs * sig)
    g_end = dot(c_t[...], (grad_y * dec_in[...]).astype(BF16)).astype(BF16)
    for i in range(NG):
        b_send[i] = g_end[i // NX * rows : (i // NX + 1) * rows, quarter(i % NX)]
    k_ab = new(NG)
    for d in range(1, NG):
        links.send(k_ab + d, b_send.at[at_m(d)], b_x.at[me], dev_m(d))
    b_x[me] = b_send[me]
    fz[...] = cols[...] * sig * (1.0 + zs * (1.0 - sig))
    for h in range(2, heads):
        span_weights(h)
    for d in range(1, ng):
        links.arrive(k_tg + d, groups.at[at_g(ng - d)], dev_g(d))

    def fall_of(i):
        return jnp.exp(tots_m[i, 0:1, :])

    def nothing():
        return jnp.zeros((rows, lanes), F32)

    for d in range(1, NG):
        links.arrive(k_ax + d, f_x.at[at_m(NG - d)], dev_m(d))
    run = nothing()
    for i in range(NG):
        f_pre[i] = run
        run = fall_of(i) * run + f_x[i].astype(F32)
    f_tot[...] = run.astype(BF16)
    k_g = new(ng)

    def send_f(d, carry):
        links.make(k_g + d, f_tot, t_g.at[mine], {"seq": (mine + d) * NG + me}).start()
        return carry

    lax.fori_loop(1, ng - mine, send_f, 0)

    for d in range(1, NG):
        links.arrive(k_ab + d, b_x.at[at_m(NG - d)], dev_m(d))
    run = nothing()
    for i in reversed(range(NG)):
        b_pre[i] = run
        run = fall_of(i) * run + b_x[i].astype(F32)
    b_tot[...] = run.astype(BF16)

    def send_b(d, carry):
        links.make(k_g + d, b_tot, t_g.at[mine], {"seq": (mine + d - ng) * NG + me}).start()
        return carry

    lax.fori_loop(ng - mine, ng, send_b, 0)

    lane = lax.broadcasted_iota(jnp.int32, (tok, lanes), 1)
    first_head = lane < head_dim
    one = lax.broadcasted_iota(jnp.int32, (1, lanes), 1)
    for q in range(NX):
        span = quarter(q)
        gain = jnp.where(one < head_dim, skip_s[2 * q], skip_s[2 * q + 1])
        xq = acc[:, span]
        xb = xq.astype(BF16)
        y_loc[:, span] = (
            jnp.where(first_head, dot(wts[2 * q], xb), dot(wts[2 * q + 1], xb)) + gain * xq
        )
        gq = grad_y[:, span]
        gb = gq.astype(BF16)
        gx_loc[:, span] = (
            jnp.where(first_head, dot(wts_t[2 * q], gb), dot(wts_t[2 * q + 1], gb)) + gain * gq
        )

    def join(i, carry):
        return jnp.exp(groups[i, 0:1, :]) * carry + t_g[i].astype(F32)

    def from_earlier(i, carry):
        links.arrive(k_g + mine - i, t_g.at[i], dev_g(1))
        return join(i, carry)

    carry = lax.fori_loop(0, mine, from_earlier, nothing())
    fall = jnp.ones((1, lanes), F32)
    for i in range(NG):
        f_back[i] = (f_pre[i] + fall * carry).astype(BF16)
        fall = fall * fall_of(i)
    k_bf = new(NG)
    for d in range(1, NG):
        links.send(k_bf + d, f_back.at[at_m(d)], f_in.at[me], dev_m(d))
    f_in[me] = f_back[me]

    def from_later(i, carry):
        source = ng - 1 - i
        links.arrive(k_g + ng + mine - source, t_g.at[source], dev_g(1))
        return join(source, carry)

    carry = lax.fori_loop(0, ng - 1 - mine, from_later, nothing())
    fall = jnp.ones((1, lanes), F32)
    for i in reversed(range(NG)):
        b_back[i] = (b_pre[i] + fall * carry).astype(BF16)
        fall = fall * fall_of(i)
    k_bb = new(NG)
    for d in range(1, NG):
        links.send(k_bb + d, b_back.at[at_m(d)], b_in.at[me], dev_m(d))
    b_in[me] = b_back[me]

    def whole(pieces, q):
        return jnp.concatenate([pieces[q + p * NX] for p in range(NP)], axis=0)

    b_all, c_all = bv[...].astype(BF16), cv[...].astype(BF16)
    for d in range(1, NG):
        links.arrive(k_bf + d, f_in.at[at_m(NG - d)], dev_m(d))
    for q in range(NX):
        span = quarter(q)
        out_y = y_loc[:, span] + dec_in[:, span] * dot(c_all, whole(f_in, q))
        gz[:, span] = (fz[:, span] * out_y).astype(BF16)
    for i, blk in enumerate((blk_o + other, blk_o)):
        for h in HALVES:
            early[2 * i + h] = dot_t(gz[...], wz[blk, h * half : (h + 1) * half, :])
    for d in range(1, NG):
        links.arrive(k_bb + d, b_in.at[at_m(NG - d)], dev_m(d))
    for q in range(NX):
        span = quarter(q)
        gx[:, span] = (gx_loc[:, span] + dec_out[:, span] * dot(b_all, whole(b_in, q))).astype(BF16)

    def share(blk, h, done):
        span = slice(h * half, (h + 1) * half)
        from_z = dot_t(gz[...], wz[blk, span, :]) if done is None else early[done + h]
        return dot_t(gx[...], wx[blk, span, :]) + from_z

    k_rs = new(8)

    def to_sib(slot, blk, h, done=None):
        s_sib[slot, h] = share(blk + other, h, done).astype(BF16)
        links.send(k_rs + 2 * slot + h, s_sib.at[slot, h], r_sib.at[slot, h], sib)

    def both(slot, blk, h, done=None):
        own = share(blk, h, done)
        links.arrive(k_rs + 2 * slot + h, r_sib.at[slot, h], sib)
        return own + r_sib[slot, h].astype(F32)

    k_or, k_ol = new(), new()
    k_er, k_el = new(2), new(2)
    to_sib(0, blk_o, LO, 0)
    to_sib(0, blk_o, HI, 0)
    to_sib(1, blk_r, HI)
    to_sib(2, blk_l, LO)
    cs_opp[LO] = both(0, blk_o, LO, 2).astype(BF16)
    links.send(k_or, cs_opp.at[LO], r_opp.at[LO], right)
    cs_opp[HI] = both(0, blk_o, HI, 2).astype(BF16)
    links.send(k_ol, cs_opp.at[HI], r_opp.at[HI], left)
    s_right[HI] = both(1, blk_r, HI).astype(BF16)
    links.send(k_er + HI, s_right.at[HI], r_left.at[HI], right)
    s_left[LO] = both(2, blk_l, LO).astype(BF16)
    links.send(k_el + LO, s_left.at[LO], r_right.at[LO], left)
    to_sib(1, blk_r, LO)
    to_sib(2, blk_l, HI)
    for h in HALVES:
        to_sib(3, head, h)
    cs_r[...] = both(1, blk_r, LO)
    cs_l[...] = both(2, blk_l, HI)
    links.arrive(k_or, r_opp.at[LO], left)
    s_right[LO] = (cs_r[...] + r_opp[LO].astype(F32)).astype(BF16)
    links.send(k_er + LO, s_right.at[LO], r_left.at[LO], right)
    links.arrive(k_ol, r_opp.at[HI], right)
    s_left[HI] = (cs_l[...] + r_opp[HI].astype(F32)).astype(BF16)
    links.send(k_el + HI, s_left.at[HI], r_right.at[HI], left)
    for h in HALVES:
        outv[h] = both(3, head, h)
    links.arrive(k_el + LO, r_right.at[LO], right)
    outv[LO] = outv[LO] + r_right[LO].astype(F32)
    links.arrive(k_er + HI, r_left.at[HI], left)
    outv[HI] = outv[HI] + r_left[HI].astype(F32)
    links.arrive(k_er + LO, r_left.at[LO], left)
    out[:, :half] = outv[LO] + r_left[LO].astype(F32)
    links.arrive(k_el + HI, r_right.at[HI], right)
    out[:, half:] = outv[HI] + r_right[HI].astype(F32)

    def sent_f(d, carry):
        links.make(k_g + d, f_tot, f_tot, dev_g(1)).wait_send()
        return carry

    lax.fori_loop(1, ng, sent_f, 0)
    links.finish()


SEMS = 96


def local(
    embedding,
    noise_draw,
    weight_x,
    weight_z,
    b_proj,
    c_proj,
    log_decay,
    skip_gain,
    class_weight,
    true_label,
):
    tok, feat = embedding.shape
    width = weight_x.shape[1]
    heads = skip_gain.shape[0]
    state = b_proj.shape[1]
    classes = class_weight.shape[1]
    n_head = lax.axis_size("head")
    nz = lax.axis_size("seq") // NX
    ny = n_head // 2
    lanes = width // NX
    half = feat // 2
    vm = pltpu.VMEM
    halves = [vm((2, tok, half), BF16)] * 2
    rows = state // NP
    eighths = [vm((NG, rows, lanes), BF16)] * 2
    scratch = [
        vm((tok, feat), BF16),
        vm((tok, feat), BF16),
        vm((n_head, feat, width), BF16),
        vm((n_head, feat, width), BF16),
        vm((tok, state), F32),
        vm((tok, state), F32),
        vm((heads, tok), F32),
        vm((classes, width), BF16),
        vm((1, tok), jnp.int32),
        vm((n_head, 2, tok, half), BF16),
        vm((tok, 2 * width), F32),
        vm((tok, width), F32),
        vm((tok, width), F32),
        vm((tok, width), F32),
        vm((heads, tok, tok), BF16),
        vm((heads, tok, tok), BF16),
        vm((state, tok), BF16),
        vm((state, tok), BF16),
        vm((NX, 8, lanes), F32),
        vm((NG, 8, lanes), F32),
        vm((8, lanes), F32),
        vm((nz // NP, 8, lanes), F32),
        *eighths,
        *eighths,
        vm((NG, rows, lanes), F32),
        vm((NG, rows, lanes), F32),
        vm((rows, lanes), BF16),
        vm((rows, lanes), BF16),
        vm((nz // NP, rows, lanes), BF16),
        *eighths,
        *eighths,
        vm((tok, width), F32),
        vm((tok, width), F32),
        vm((tok, width), F32),
        vm((tok, width), BF16),
        vm((tok, width), BF16),
        vm((4, 2, tok, half), BF16),
        vm((4, 2, tok, half), BF16),
        *halves,
        vm((tok, half), F32),
        vm((tok, half), F32),
        *halves,
        *halves,
        vm((2, tok, half), F32),
        vm((4, tok, half), F32),
        pltpu.SemaphoreType.DMA((9,)),
        pltpu.SemaphoreType.REGULAR((3,)),
        pltpu.SemaphoreType.DMA((SEMS,)),
        pltpu.SemaphoreType.DMA((SEMS,)),
    ]
    anywhere = pl.BlockSpec(memory_space=pl.ANY)
    return pl.pallas_call(
        functools.partial(kernel, nz, ny),
        out_shape=pltpu.VMEM((tok, feat), F32),
        in_specs=[anywhere] * 9 + [pl.BlockSpec(memory_space=pltpu.SMEM)],
        out_specs=pl.BlockSpec(memory_space=pltpu.VMEM),
        scratch_shapes=scratch,
        compiler_params=pltpu.CompilerParams(
            collective_id=0, has_side_effects=True, vmem_limit_bytes=60 * 1024 * 1024
        ),
        cost_estimate=pl.CostEstimate(
            flops=8 * tok * feat * n_head * width,
            bytes_accessed=10 * 1024 * 1024,
            transcendentals=heads * tok * tok * 2,
        ),
    )(
        embedding,
        noise_draw,
        weight_x.reshape(n_head, feat, width),
        weight_z.reshape(n_head, feat, width),
        b_proj,
        c_proj,
        log_decay,
        class_weight.T,
        true_label.reshape(1, tok),
        skip_gain,
    )


def solution(mesh):
    return jax.shard_map(
        local,
        mesh=mesh,
        in_specs=(
            P("seq", "head"),
            P("seq", "head"),
            P(None, "head"),
            P(None, "head"),
            P("seq", None),
            P("seq", None),
            P("head", "seq"),
            P("head"),
            P("head", None),
            P("seq"),
        ),
        out_specs=P("seq", "head"),
        check_vma=False,
    )
```

```python
import functools

import jax
import jax.numpy as jnp
from jax import lax
from jax.experimental import pallas as pl
from jax.experimental.pallas import tpu as pltpu
from jax.sharding import PartitionSpec as P

F32 = jnp.float32
BF16 = jnp.bfloat16
MESH = pl.DeviceIdType.MESH
NX = 4
NP = 2
NG = NP * NX
PRECISE = lax.Precision.HIGHEST
LO, HI = 0, 1
HALVES = (LO, HI)


def dot(a, b):
    return jnp.dot(a, b, preferred_element_type=F32)


def dot_t(a, b, precision=None):
    return lax.dot_general(
        a, b, (((1,), (1,)), ((), ())), preferred_element_type=F32, precision=precision
    )


class Links:
    def __init__(self, send_sems, recv_sems):
        self.send_sems, self.recv_sems = send_sems, recv_sems
        self.sent = []

    def make(self, k, src, dst, device):
        return pltpu.make_async_remote_copy(
            src_ref=src,
            dst_ref=dst,
            send_sem=self.send_sems.at[k],
            recv_sem=self.recv_sems.at[k],
            device_id=device,
            device_id_type=MESH,
        )

    def send(self, k, src, dst, device):
        copy = self.make(k, src, dst, device)
        copy.start()
        self.sent.append(copy)

    def arrive(self, k, dst, device):
        self.make(k, dst, dst, device).wait_recv()

    def finish(self):
        for copy in self.sent:
            copy.wait_send()


def kernel(
    nz,
    ny,
    emb_h,
    noise_h,
    wx_h,
    wz_h,
    b_h,
    c_h,
    ld_h,
    cw_h,
    lab_h,
    skip_h,
    out,
    ev,
    nv,
    wx,
    wz,
    bv,
    cv,
    ldv,
    cwv,
    labv,
    skipv,
    mix,
    acc,
    dec_in,
    dec_out,
    cols,
    wts,
    wts_t,
    b_t,
    c_t,
    tots,
    tots_m,
    group,
    groups,
    f_send,
    b_send,
    f_x,
    b_x,
    f_pre,
    b_pre,
    f_tot,
    b_tot,
    t_g,
    f_back,
    b_back,
    f_in,
    b_in,
    y_loc,
    gx_loc,
    fz,
    gx,
    gz,
    s_sib,
    r_sib,
    cs_opp,
    r_opp,
    cs_r,
    cs_l,
    s_right,
    s_left,
    r_left,
    r_right,
    outv,
    early,
    local_sems,
    relay,
    send_sems,
    recv_sems,
):
    tok, feat = ev.shape
    half = feat // 2
    width = acc.shape[1] // 2
    heads = ldv.shape[0]
    head_dim = width // heads
    state = bv.shape[1]
    lanes = width // NX
    seq, head = lax.axis_index("seq"), lax.axis_index("head")
    z, x = seq // NX, seq % NX
    y, core = head // 2, head % 2
    other = 1 - 2 * core

    links = Links(send_sems, recv_sems)
    counter = [0]

    def new(count=1):
        first = counter[0]
        counter[0] += count
        return first

    pairs = [
        (emb_h, ev),
        (noise_h, nv),
        (ld_h, ldv),
        (b_h, bv),
        (c_h, cv),
        (cw_h, cwv),
        (lab_h, labv),
        (skip_h, skipv),
        (wx_h, wx),
        (wz_h, wz),
    ]
    loads = [pltpu.make_async_copy(s, d, local_sems.at[i]) for i, (s, d) in enumerate(pairs)]
    for load in loads:
        load.start()

    sib = {"head": head + other}
    blk_r = ((y + 1) % ny) * 2 + core
    blk_l = ((y + ny - 1) % ny) * 2 + core
    blk_o = ((y + 2) % ny) * 2 + core
    right, left = {"head": blk_r}, {"head": blk_l}

    ng = nz // NP
    me, mine = (z % NP) * NX + x, z // NP

    def at_m(d):
        return (me + d) % NG

    def at_g(d):
        return (mine + d) % ng

    def dev_m(d):
        return {"seq": mine * NG + at_m(d)}

    def dev_g(d):
        return {"seq": at_g(d) * NG + me}

    barrier = pltpu.get_barrier_semaphore()
    near = [{"seq": z * NX + (x + d) % NX} for d in (1, NX - 1)]
    near += [{"seq": (z + d) % nz * NX + x} for d in (1, nz - 1)]
    partners = [sib, right, left] + near
    for partner in partners:
        pl.semaphore_signal(barrier, inc=1, device_id=partner, device_id_type=MESH)

    def tell(r):
        for partner in near:
            pl.semaphore_signal(relay.at[r], inc=1, device_id=partner, device_id_type=MESH)

    def told(r):
        pl.semaphore_wait(relay.at[r], len(near))

    loads[0].wait()
    loads[1].wait()
    noisy = (ev[...].astype(F32) + nv[...].astype(F32)).astype(BF16)
    for h in HALVES:
        mix[head, h] = noisy[:, h * half : (h + 1) * half]
    pl.semaphore_wait(barrier, len(partners))

    def piece(blk, h):
        return mix.at[blk, h]

    k_r, k_l, k_own = new(2), new(2), new()
    k_fr, k_fl = new(), new()
    k_sib = {name: new(2) for name in ("l", "r", "o")}

    def hand_on(name, blk, h):
        links.send(k_sib[name] + h, piece(blk, h), piece(blk, h), sib)

    def from_sib(name, blk, h):
        links.arrive(k_sib[name] + h, piece(blk, h), sib)

    links.send(k_r + LO, piece(head, LO), piece(head, LO), right)
    links.send(k_l + HI, piece(head, HI), piece(head, HI), left)
    links.send(k_own, mix.at[head], mix.at[head], sib)
    links.send(k_r + HI, piece(head, HI), piece(head, HI), right)
    links.send(k_l + LO, piece(head, LO), piece(head, LO), left)
    tell(0)

    loads[2].wait()
    rates = ldv[...]
    ones_t = lax.broadcasted_iota(jnp.int32, (tok, tok), 0)
    ones_s = lax.broadcasted_iota(jnp.int32, (tok, tok), 1)
    lower = ones_t >= ones_s
    tri = jnp.where(lower, 1.0, 0.0).astype(F32)
    tri_t = jnp.where(ones_s >= ones_t, 1.0, 0.0).astype(F32)
    cum_row = jnp.dot(rates, tri_t, preferred_element_type=F32, precision=PRECISE)
    wide = jnp.concatenate(
        [jnp.broadcast_to(rates[h : h + 1, :], (head_dim, tok)) for h in range(heads)], axis=0
    )
    cum = dot_t(tri, wide, PRECISE)
    total = cum[tok - 1 : tok, :]
    dec_in[...] = jnp.exp(cum)
    dec_out[...] = jnp.exp(total - cum)
    for q in range(NX):
        tots[q] = jnp.broadcast_to(total[:, q * lanes : (q + 1) * lanes], (8, lanes))
    tots_m[me] = tots[x]
    told(0)
    tell(1)

    links.arrive(k_r + LO, piece(blk_l, LO), left)
    links.send(k_fr, piece(blk_l, LO), piece(blk_l, LO), right)
    hand_on("l", blk_l, LO)
    links.arrive(k_l + HI, piece(blk_r, HI), right)
    links.send(k_fl, piece(blk_r, HI), piece(blk_r, HI), left)
    hand_on("r", blk_r, HI)
    told(1)
    tell(2)
    k_tm = new(NG)
    for d in range(1, NG):
        links.send(k_tm + d, tots.at[at_m(d) % NX], tots_m.at[me], dev_m(d))

    loads[5].wait()
    loads[6].wait()
    classes = cwv.shape[0]
    is_label = lax.broadcasted_iota(jnp.int32, (128, tok), 0) == labv[...]
    onehot = jnp.where(is_label, 1.0, 0.0).astype(F32).T[:, :classes].astype(BF16)
    cols[...] = dot(onehot, cwv[...])

    loads[3].wait()
    loads[4].wait()
    b_all, c_all = bv[...], cv[...]
    scores = dot_t(c_all, b_all, PRECISE)
    scores_t = dot_t(b_all, c_all, PRECISE)
    b_t[...] = b_all.T.astype(BF16)
    c_t[...] = c_all.T.astype(BF16)

    def span_weights(h):
        down = jnp.broadcast_to(cum[:, h * head_dim : h * head_dim + 1], (tok, tok))
        across = jnp.broadcast_to(cum_row[h : h + 1, :], (tok, tok))
        fall = jnp.exp(jnp.minimum(down - across, 0.0))
        wts[h] = (jnp.where(lower, fall, 0.0) * scores).astype(BF16)
        rise = jnp.exp(jnp.minimum(across - down, 0.0))
        wts_t[h] = (jnp.where(ones_s >= ones_t, rise, 0.0) * scores_t).astype(BF16)

    def project(blk, h, first=False):
        m = mix[blk, h]
        for i, w in enumerate((wx, wz)):
            span = slice(i * width, (i + 1) * width)
            term = dot(m, w[blk, h * half : (h + 1) * half, :])
            acc[:, span] = term if first else acc[:, span] + term

    for h in range(0, 2):
        span_weights(h)
    loads[8].wait()
    loads[9].wait()
    project(head, LO, True)
    project(head, HI)

    links.arrive(k_own, mix.at[head + other], sib)
    links.arrive(k_r + HI, piece(blk_l, HI), left)
    hand_on("l", blk_l, HI)
    links.arrive(k_l + LO, piece(blk_r, LO), right)
    hand_on("r", blk_r, LO)
    for h in HALVES:
        project(head + other, h)

    for h in HALVES:
        project(blk_l, h)
        project(blk_r, h)
    for h in HALVES:
        from_sib("l", blk_l + other, h)
        project(blk_l + other, h)
        from_sib("r", blk_r + other, h)
        project(blk_r + other, h)

    links.arrive(k_fr, piece(blk_o, LO), left)
    hand_on("o", blk_o, LO)
    links.arrive(k_fl, piece(blk_o, HI), right)
    hand_on("o", blk_o, HI)
    for h in HALVES:
        project(blk_o, h)
    for h in HALVES:
        from_sib("o", blk_o + other, h)
        project(blk_o + other, h)

    def quarter(q):
        return slice(q * lanes, (q + 1) * lanes)

    xs = acc[:, :width]
    x_end = dot(b_t[...], (xs * dec_out[...]).astype(BF16)).astype(BF16)
    rows = state // NP
    for i in range(NG):
        f_send[i] = x_end[i // NX * rows : (i // NX + 1) * rows, quarter(i % NX)]
    k_ax = new(NG)
    for d in range(1, NG):
        links.send(k_ax + d, f_send.at[at_m(d)], f_x.at[me], dev_m(d))
    f_x[me] = f_send[me]

    zs = acc[:, width:]
    sig = jax.nn.sigmoid(zs)
    grad_y = cols[...] * (zs * sig)
    g_end = dot(c_t[...], (grad_y * dec_in[...]).astype(BF16)).astype(BF16)
    for i in range(NG):
        b_send[i] = g_end[i // NX * rows : (i // NX + 1) * rows, quarter(i % NX)]
    k_ab = new(NG)
    for d in range(1, NG):
        links.send(k_ab + d, b_send.at[at_m(d)], b_x.at[me], dev_m(d))
    b_x[me] = b_send[me]
    fz[...] = cols[...] * sig * (1.0 + zs * (1.0 - sig))
    for d in range(1, NG):
        links.arrive(k_tm + d, tots_m.at[at_m(NG - d)], dev_m(d))
    group[...] = functools.reduce(lambda a, b: a + b, [tots_m[i] for i in range(NG)])
    told(2)
    k_tg = new(ng)
    for d in range(1, ng):
        links.send(k_tg + d, group, groups.at[mine], dev_g(d))
    for h in range(2, heads):
        span_weights(h)

    def fall_of(i):
        return jnp.exp(tots_m[i, 0:1, :])

    def nothing():
        return jnp.zeros((rows, lanes), F32)

    for d in range(1, NG):
        links.arrive(k_ax + d, f_x.at[at_m(NG - d)], dev_m(d))
    run = nothing()
    for i in range(NG):
        f_pre[i] = run
        run = fall_of(i) * run + f_x[i].astype(F32)
    f_tot[...] = run.astype(BF16)
    k_g = new(ng)

    def send_f(d, carry):
        links.make(k_g + d, f_tot, t_g.at[mine], {"seq": (mine + d) * NG + me}).start()
        return carry

    lax.fori_loop(1, ng - mine, send_f, 0)

    for d in range(1, NG):
        links.arrive(k_ab + d, b_x.at[at_m(NG - d)], dev_m(d))
    run = nothing()
    for i in reversed(range(NG)):
        b_pre[i] = run
        run = fall_of(i) * run + b_x[i].astype(F32)
    b_tot[...] = run.astype(BF16)

    def send_b(d, carry):
        links.make(k_g + d, b_tot, t_g.at[mine], {"seq": (mine + d - ng) * NG + me}).start()
        return carry

    lax.fori_loop(ng - mine, ng, send_b, 0)

    lane = lax.broadcasted_iota(jnp.int32, (tok, lanes), 1)
    first_head = lane < head_dim
    one = lax.broadcasted_iota(jnp.int32, (1, lanes), 1)
    loads[7].wait()
    gains = skipv[...]
    for q in range(NX):
        span = quarter(q)
        gain = jnp.where(one < head_dim, gains[:, 2 * q : 2 * q + 1], gains[:, 2 * q + 1 : 2 * q + 2])
        xq = acc[:, span]
        xb = xq.astype(BF16)
        y_loc[:, span] = (
            jnp.where(first_head, dot(wts[2 * q], xb), dot(wts[2 * q + 1], xb)) + gain * xq
        )
        gq = grad_y[:, span]
        gb = gq.astype(BF16)
        gx_loc[:, span] = (
            jnp.where(first_head, dot(wts_t[2 * q], gb), dot(wts_t[2 * q + 1], gb)) + gain * gq
        )

    for d in range(1, ng):
        links.arrive(k_tg + d, groups.at[at_g(ng - d)], dev_g(d))

    def join(i, carry):
        return jnp.exp(groups[i, 0:1, :]) * carry + t_g[i].astype(F32)

    def from_earlier(i, carry):
        links.arrive(k_g + mine - i, t_g.at[i], dev_g(1))
        return join(i, carry)

    carry = lax.fori_loop(0, mine, from_earlier, nothing())
    fall = jnp.ones((1, lanes), F32)
    for i in range(NG):
        f_back[i] = (f_pre[i] + fall * carry).astype(BF16)
        fall = fall * fall_of(i)
    k_bf = new(NG)
    for d in range(1, NG):
        links.send(k_bf + d, f_back.at[at_m(d)], f_in.at[me], dev_m(d))
    f_in[me] = f_back[me]

    def from_later(i, carry):
        source = ng - 1 - i
        links.arrive(k_g + ng + mine - source, t_g.at[source], dev_g(1))
        return join(source, carry)

    carry = lax.fori_loop(0, ng - 1 - mine, from_later, nothing())
    fall = jnp.ones((1, lanes), F32)
    for i in reversed(range(NG)):
        b_back[i] = (b_pre[i] + fall * carry).astype(BF16)
        fall = fall * fall_of(i)
    k_bb = new(NG)
    for d in range(1, NG):
        links.send(k_bb + d, b_back.at[at_m(d)], b_in.at[me], dev_m(d))
    b_in[me] = b_back[me]

    def whole(pieces, q):
        return jnp.concatenate([pieces[q + p * NX] for p in range(NP)], axis=0)

    b_all, c_all = bv[...].astype(BF16), cv[...].astype(BF16)
    for d in range(1, NG):
        links.arrive(k_bf + d, f_in.at[at_m(NG - d)], dev_m(d))
    for q in range(NX):
        span = quarter(q)
        out_y = y_loc[:, span] + dec_in[:, span] * dot(c_all, whole(f_in, q))
        gz[:, span] = (fz[:, span] * out_y).astype(BF16)
    for i, blk in enumerate((blk_o + other, blk_o)):
        for h in HALVES:
            early[2 * i + h] = dot_t(gz[...], wz[blk, h * half : (h + 1) * half, :])
    for d in range(1, NG):
        links.arrive(k_bb + d, b_in.at[at_m(NG - d)], dev_m(d))
    for q in range(NX):
        span = quarter(q)
        gx[:, span] = (gx_loc[:, span] + dec_out[:, span] * dot(b_all, whole(b_in, q))).astype(BF16)

    def share(blk, h, done):
        span = slice(h * half, (h + 1) * half)
        from_z = dot_t(gz[...], wz[blk, span, :]) if done is None else early[done + h]
        return dot_t(gx[...], wx[blk, span, :]) + from_z

    k_rs = new(8)

    def to_sib(slot, blk, h, done=None):
        s_sib[slot, h] = share(blk + other, h, done).astype(BF16)
        links.send(k_rs + 2 * slot + h, s_sib.at[slot, h], r_sib.at[slot, h], sib)

    def both(slot, blk, h, done=None):
        own = share(blk, h, done)
        links.arrive(k_rs + 2 * slot + h, r_sib.at[slot, h], sib)
        return own + r_sib[slot, h].astype(F32)

    k_or, k_ol = new(), new()
    k_er, k_el = new(2), new(2)
    to_sib(0, blk_o, LO, 0)
    to_sib(0, blk_o, HI, 0)
    to_sib(1, blk_r, HI)
    to_sib(2, blk_l, LO)
    cs_opp[LO] = both(0, blk_o, LO, 2).astype(BF16)
    links.send(k_or, cs_opp.at[LO], r_opp.at[LO], right)
    cs_opp[HI] = both(0, blk_o, HI, 2).astype(BF16)
    links.send(k_ol, cs_opp.at[HI], r_opp.at[HI], left)
    s_right[HI] = both(1, blk_r, HI).astype(BF16)
    links.send(k_er + HI, s_right.at[HI], r_left.at[HI], right)
    s_left[LO] = both(2, blk_l, LO).astype(BF16)
    links.send(k_el + LO, s_left.at[LO], r_right.at[LO], left)
    to_sib(1, blk_r, LO)
    to_sib(2, blk_l, HI)
    for h in HALVES:
        to_sib(3, head, h)
    cs_r[...] = both(1, blk_r, LO)
    cs_l[...] = both(2, blk_l, HI)
    links.arrive(k_or, r_opp.at[LO], left)
    s_right[LO] = (cs_r[...] + r_opp[LO].astype(F32)).astype(BF16)
    links.send(k_er + LO, s_right.at[LO], r_left.at[LO], right)
    links.arrive(k_ol, r_opp.at[HI], right)
    s_left[HI] = (cs_l[...] + r_opp[HI].astype(F32)).astype(BF16)
    links.send(k_el + HI, s_left.at[HI], r_right.at[HI], left)
    for h in HALVES:
        outv[h] = both(3, head, h)
    links.arrive(k_el + LO, r_right.at[LO], right)
    outv[LO] = outv[LO] + r_right[LO].astype(F32)
    links.arrive(k_er + HI, r_left.at[HI], left)
    outv[HI] = outv[HI] + r_left[HI].astype(F32)
    links.arrive(k_er + LO, r_left.at[LO], left)
    out[:, :half] = outv[LO] + r_left[LO].astype(F32)
    links.arrive(k_el + HI, r_right.at[HI], right)
    out[:, half:] = outv[HI] + r_right[HI].astype(F32)

    def sent_f(d, carry):
        links.make(k_g + d, f_tot, f_tot, dev_g(1)).wait_send()
        return carry

    lax.fori_loop(1, ng, sent_f, 0)
    links.finish()


SEMS = 96


def local(
    embedding,
    noise_draw,
    weight_x,
    weight_z,
    b_proj,
    c_proj,
    log_decay,
    skip_gain,
    class_weight,
    true_label,
):
    tok, feat = embedding.shape
    width = weight_x.shape[1]
    heads = skip_gain.shape[0]
    state = b_proj.shape[1]
    classes = class_weight.shape[1]
    n_head = lax.axis_size("head")
    nz = lax.axis_size("seq") // NX
    ny = n_head // 2
    lanes = width // NX
    half = feat // 2
    vm = pltpu.VMEM
    halves = [vm((2, tok, half), BF16)] * 2
    rows = state // NP
    eighths = [vm((NG, rows, lanes), BF16)] * 2
    scratch = [
        vm((tok, feat), BF16),
        vm((tok, feat), BF16),
        vm((n_head, feat, width), BF16),
        vm((n_head, feat, width), BF16),
        vm((tok, state), F32),
        vm((tok, state), F32),
        vm((heads, tok), F32),
        vm((classes, width), BF16),
        vm((1, tok), jnp.int32),
        vm((1, heads), F32),
        vm((n_head, 2, tok, half), BF16),
        vm((tok, 2 * width), F32),
        vm((tok, width), F32),
        vm((tok, width), F32),
        vm((tok, width), F32),
        vm((heads, tok, tok), BF16),
        vm((heads, tok, tok), BF16),
        vm((state, tok), BF16),
        vm((state, tok), BF16),
        vm((NX, 8, lanes), F32),
        vm((NG, 8, lanes), F32),
        vm((8, lanes), F32),
        vm((nz // NP, 8, lanes), F32),
        *eighths,
        *eighths,
        vm((NG, rows, lanes), F32),
        vm((NG, rows, lanes), F32),
        vm((rows, lanes), BF16),
        vm((rows, lanes), BF16),
        vm((nz // NP, rows, lanes), BF16),
        *eighths,
        *eighths,
        vm((tok, width), F32),
        vm((tok, width), F32),
        vm((tok, width), F32),
        vm((tok, width), BF16),
        vm((tok, width), BF16),
        vm((4, 2, tok, half), BF16),
        vm((4, 2, tok, half), BF16),
        *halves,
        vm((tok, half), F32),
        vm((tok, half), F32),
        *halves,
        *halves,
        vm((2, tok, half), F32),
        vm((4, tok, half), F32),
        pltpu.SemaphoreType.DMA((10,)),
        pltpu.SemaphoreType.REGULAR((3,)),
        pltpu.SemaphoreType.DMA((SEMS,)),
        pltpu.SemaphoreType.DMA((SEMS,)),
    ]
    anywhere = pl.BlockSpec(memory_space=pl.ANY)
    return pl.pallas_call(
        functools.partial(kernel, nz, ny),
        out_shape=pltpu.VMEM((tok, feat), F32),
        in_specs=[anywhere] * 10,
        out_specs=pl.BlockSpec(memory_space=pltpu.VMEM),
        scratch_shapes=scratch,
        compiler_params=pltpu.CompilerParams(
            collective_id=0, has_side_effects=True, vmem_limit_bytes=60 * 1024 * 1024
        ),
        cost_estimate=pl.CostEstimate(
            flops=8 * tok * feat * n_head * width,
            bytes_accessed=10 * 1024 * 1024,
            transcendentals=heads * tok * tok * 2,
        ),
    )(
        embedding,
        noise_draw,
        weight_x.reshape(n_head, feat, width),
        weight_z.reshape(n_head, feat, width),
        b_proj,
        c_proj,
        log_decay,
        class_weight.T,
        true_label.reshape(1, tok),
        skip_gain.reshape(1, heads),
    )


def solution(mesh):
    return jax.shard_map(
        local,
        mesh=mesh,
        in_specs=(
            P("seq", "head"),
            P("seq", "head"),
            P(None, "head"),
            P(None, "head"),
            P("seq", None),
            P("seq", None),
            P("head", "seq"),
            P("head"),
            P("head", None),
            P("seq"),
        ),
        out_specs=P("seq", "head"),
        check_vma=False,
    )
```

```python
import functools

import jax
import jax.numpy as jnp
from jax import lax
from jax.experimental import pallas as pl
from jax.experimental.pallas import tpu as pltpu
from jax.sharding import PartitionSpec as P

F32 = jnp.float32
BF16 = jnp.bfloat16
MESH = pl.DeviceIdType.MESH
NX = 4
NP = 2
NG = NP * NX
PRECISE = lax.Precision.HIGHEST
LO, HI = 0, 1
HALVES = (LO, HI)


def dot(a, b):
    return jnp.dot(a, b, preferred_element_type=F32)


def dot_t(a, b, precision=None):
    return lax.dot_general(
        a, b, (((1,), (1,)), ((), ())), preferred_element_type=F32, precision=precision
    )


class Links:
    def __init__(self, send_sems, recv_sems):
        self.send_sems, self.recv_sems = send_sems, recv_sems
        self.sent = []

    def make(self, k, src, dst, device):
        return pltpu.make_async_remote_copy(
            src_ref=src,
            dst_ref=dst,
            send_sem=self.send_sems.at[k],
            recv_sem=self.recv_sems.at[k],
            device_id=device,
            device_id_type=MESH,
        )

    def send(self, k, src, dst, device):
        copy = self.make(k, src, dst, device)
        copy.start()
        self.sent.append(copy)

    def arrive(self, k, dst, device):
        self.make(k, dst, dst, device).wait_recv()

    def finish(self):
        for copy in self.sent:
            copy.wait_send()


def kernel(
    nz,
    ny,
    emb_h,
    noise_h,
    wx_h,
    wz_h,
    b_h,
    c_h,
    ld_h,
    cw_h,
    lab_h,
    skip_h,
    out,
    ev,
    nv,
    wx,
    wz,
    bv,
    cv,
    ldv,
    cwv,
    labv,
    skipv,
    mix,
    acc,
    dec_in,
    dec_out,
    cols,
    wts,
    wts_t,
    b_t,
    c_t,
    tots,
    tots_m,
    group,
    groups,
    f_send,
    b_send,
    f_x,
    b_x,
    f_pre,
    b_pre,
    f_tot,
    b_tot,
    t_g,
    f_back,
    b_back,
    f_in,
    b_in,
    y_loc,
    gx_loc,
    fz,
    gx,
    gz,
    s_sib,
    r_sib,
    cs_opp,
    r_opp,
    cs_r,
    cs_l,
    s_right,
    s_left,
    r_left,
    r_right,
    outv,
    early,
    local_sems,
    relay,
    send_sems,
    recv_sems,
):
    tok, feat = ev.shape
    half = feat // 2
    width = acc.shape[1] // 2
    heads = ldv.shape[0]
    head_dim = width // heads
    state = bv.shape[1]
    lanes = width // NX
    seq, head = lax.axis_index("seq"), lax.axis_index("head")
    z, x = seq // NX, seq % NX
    y, core = head // 2, head % 2
    other = 1 - 2 * core

    links = Links(send_sems, recv_sems)
    counter = [0]

    def new(count=1):
        first = counter[0]
        counter[0] += count
        return first

    pairs = [
        (emb_h, ev),
        (noise_h, nv),
        (ld_h, ldv),
        (b_h, bv),
        (c_h, cv),
        (cw_h, cwv),
        (lab_h, labv),
        (skip_h, skipv),
        (wx_h, wx),
        (wz_h, wz),
    ]
    loads = [pltpu.make_async_copy(s, d, local_sems.at[i]) for i, (s, d) in enumerate(pairs)]
    for load in loads:
        load.start()

    sib = {"head": head + other}
    blk_r = ((y + 1) % ny) * 2 + core
    blk_l = ((y + ny - 1) % ny) * 2 + core
    blk_o = ((y + 2) % ny) * 2 + core
    right, left = {"head": blk_r}, {"head": blk_l}

    ng = nz // NP
    me, mine = (z % NP) * NX + x, z // NP

    def at_m(d):
        return (me + d) % NG

    def at_g(d):
        return (mine + d) % ng

    def dev_m(d):
        return {"seq": mine * NG + at_m(d)}

    def dev_g(d):
        return {"seq": at_g(d) * NG + me}

    barrier = pltpu.get_barrier_semaphore()
    near = [{"seq": z * NX + (x + d) % NX} for d in (1, NX - 1)]
    near += [{"seq": (z + d) % nz * NX + x} for d in (1, nz - 1)]
    partners = [sib, right, left] + near
    for partner in partners:
        pl.semaphore_signal(barrier, inc=1, device_id=partner, device_id_type=MESH)

    def tell(r):
        for partner in near:
            pl.semaphore_signal(relay.at[r], inc=1, device_id=partner, device_id_type=MESH)

    def told(r):
        pl.semaphore_wait(relay.at[r], len(near))

    loads[0].wait()
    loads[1].wait()
    noisy = (ev[...].astype(F32) + nv[...].astype(F32)).astype(BF16)
    for h in HALVES:
        mix[head, h] = noisy[:, h * half : (h + 1) * half]
    pl.semaphore_wait(barrier, len(partners))

    def piece(blk, h):
        return mix.at[blk, h]

    k_r, k_l, k_own = new(2), new(2), new()
    k_fr, k_fl = new(), new()
    k_sib = {name: new(2) for name in ("l", "r", "o")}

    def hand_on(name, blk, h):
        links.send(k_sib[name] + h, piece(blk, h), piece(blk, h), sib)

    def from_sib(name, blk, h):
        links.arrive(k_sib[name] + h, piece(blk, h), sib)

    links.send(k_r + LO, piece(head, LO), piece(head, LO), right)
    links.send(k_l + HI, piece(head, HI), piece(head, HI), left)
    links.send(k_own, mix.at[head], mix.at[head], sib)
    links.send(k_r + HI, piece(head, HI), piece(head, HI), right)
    links.send(k_l + LO, piece(head, LO), piece(head, LO), left)
    tell(0)

    loads[2].wait()
    rates = ldv[...]
    ones_t = lax.broadcasted_iota(jnp.int32, (tok, tok), 0)
    ones_s = lax.broadcasted_iota(jnp.int32, (tok, tok), 1)
    lower = ones_t >= ones_s
    tri = jnp.where(lower, 1.0, 0.0).astype(F32)
    tri_t = jnp.where(ones_s >= ones_t, 1.0, 0.0).astype(F32)
    cum_row = jnp.dot(rates, tri_t, preferred_element_type=F32, precision=PRECISE)
    wide = jnp.concatenate(
        [jnp.broadcast_to(rates[h : h + 1, :], (head_dim, tok)) for h in range(heads)], axis=0
    )
    cum = dot_t(tri, wide, PRECISE)
    total = cum[tok - 1 : tok, :]
    dec_in[...] = jnp.exp(cum)
    dec_out[...] = jnp.exp(total - cum)
    for q in range(NX):
        tots[q] = jnp.broadcast_to(total[:, q * lanes : (q + 1) * lanes], (8, lanes))
    tots_m[me] = tots[x]
    told(0)
    tell(1)

    links.arrive(k_r + LO, piece(blk_l, LO), left)
    links.send(k_fr, piece(blk_l, LO), piece(blk_l, LO), right)
    hand_on("l", blk_l, LO)
    links.arrive(k_l + HI, piece(blk_r, HI), right)
    links.send(k_fl, piece(blk_r, HI), piece(blk_r, HI), left)
    hand_on("r", blk_r, HI)
    told(1)
    tell(2)
    k_tm = new(NG)
    for d in range(1, NG):
        links.send(k_tm + d, tots.at[at_m(d) % NX], tots_m.at[me], dev_m(d))

    loads[5].wait()
    loads[6].wait()
    classes = cwv.shape[0]
    is_label = lax.broadcasted_iota(jnp.int32, (128, tok), 0) == labv[...]
    onehot = jnp.where(is_label, 1.0, 0.0).astype(F32).T[:, :classes].astype(BF16)
    cols[...] = dot(onehot, cwv[...])

    loads[3].wait()
    loads[4].wait()
    b_all, c_all = bv[...], cv[...]
    scores = dot_t(c_all, b_all, PRECISE)
    scores_t = dot_t(b_all, c_all, PRECISE)
    b_t[...] = b_all.T.astype(BF16)
    c_t[...] = c_all.T.astype(BF16)

    def span_weights(h):
        down = jnp.broadcast_to(cum[:, h * head_dim : h * head_dim + 1], (tok, tok))
        across = jnp.broadcast_to(cum_row[h : h + 1, :], (tok, tok))
        fall = jnp.exp(jnp.minimum(down - across, 0.0))
        wts[h] = (jnp.where(lower, fall, 0.0) * scores).astype(BF16)
        rise = jnp.exp(jnp.minimum(across - down, 0.0))
        wts_t[h] = (jnp.where(ones_s >= ones_t, rise, 0.0) * scores_t).astype(BF16)

    def project(blk, h, first=False):
        m = mix[blk, h]
        for i, w in enumerate((wx, wz)):
            span = slice(i * width, (i + 1) * width)
            term = dot(m, w[blk, h * half : (h + 1) * half, :])
            acc[:, span] = term if first else acc[:, span] + term

    for h in range(0, 2):
        span_weights(h)
    loads[8].wait()
    loads[9].wait()
    project(head, LO, True)
    project(head, HI)

    links.arrive(k_own, mix.at[head + other], sib)
    links.arrive(k_r + HI, piece(blk_l, HI), left)
    hand_on("l", blk_l, HI)
    links.arrive(k_l + LO, piece(blk_r, LO), right)
    hand_on("r", blk_r, LO)
    for h in HALVES:
        project(head + other, h)

    for h in HALVES:
        project(blk_l, h)
        project(blk_r, h)
    for h in HALVES:
        from_sib("l", blk_l + other, h)
        project(blk_l + other, h)
        from_sib("r", blk_r + other, h)
        project(blk_r + other, h)

    links.arrive(k_fr, piece(blk_o, LO), left)
    hand_on("o", blk_o, LO)
    links.arrive(k_fl, piece(blk_o, HI), right)
    hand_on("o", blk_o, HI)
    for h in HALVES:
        project(blk_o, h)
    for h in HALVES:
        from_sib("o", blk_o + other, h)
        project(blk_o + other, h)

    def quarter(q):
        return slice(q * lanes, (q + 1) * lanes)

    xs = acc[:, :width]
    x_end = dot(b_t[...], (xs * dec_out[...]).astype(BF16)).astype(BF16)
    rows = state // NP
    for i in range(NG):
        f_send[i] = x_end[i // NX * rows : (i // NX + 1) * rows, quarter(i % NX)]
    k_ax = new(NG)
    for d in range(1, NG):
        links.send(k_ax + d, f_send.at[at_m(d)], f_x.at[me], dev_m(d))
    f_x[me] = f_send[me]

    zs = acc[:, width:]
    sig = jax.nn.sigmoid(zs)
    grad_y = cols[...] * (zs * sig)
    g_end = dot(c_t[...], (grad_y * dec_in[...]).astype(BF16)).astype(BF16)
    for i in range(NG):
        b_send[i] = g_end[i // NX * rows : (i // NX + 1) * rows, quarter(i % NX)]
    k_ab = new(NG)
    for d in range(1, NG):
        links.send(k_ab + d, b_send.at[at_m(d)], b_x.at[me], dev_m(d))
    b_x[me] = b_send[me]
    fz[...] = cols[...] * sig * (1.0 + zs * (1.0 - sig))
    for d in range(1, NG):
        links.arrive(k_tm + d, tots_m.at[at_m(NG - d)], dev_m(d))
    group[...] = functools.reduce(lambda a, b: a + b, [tots_m[i] for i in range(NG)])
    told(2)
    k_tg = new(ng)
    for d in range(1, ng):
        links.send(k_tg + d, group, groups.at[mine], dev_g(d))
    for h in range(2, heads):
        span_weights(h)

    def fall_of(i):
        return jnp.exp(tots_m[i, 0:1, :])

    def nothing():
        return jnp.zeros((rows, lanes), F32)

    for d in range(1, NG):
        links.arrive(k_ax + d, f_x.at[at_m(NG - d)], dev_m(d))
    run = nothing()
    for i in range(NG):
        f_pre[i] = run
        run = fall_of(i) * run + f_x[i].astype(F32)
    f_tot[...] = run.astype(BF16)
    k_g = new(ng)

    def send_f(d, carry):
        links.make(k_g + d, f_tot, t_g.at[mine], {"seq": (mine + d) * NG + me}).start()
        return carry

    lax.fori_loop(1, ng - mine, send_f, 0)

    for d in range(1, NG):
        links.arrive(k_ab + d, b_x.at[at_m(NG - d)], dev_m(d))
    run = nothing()
    for i in reversed(range(NG)):
        b_pre[i] = run
        run = fall_of(i) * run + b_x[i].astype(F32)
    b_tot[...] = run.astype(BF16)

    def send_b(d, carry):
        links.make(k_g + d, b_tot, t_g.at[mine], {"seq": (mine + d - ng) * NG + me}).start()
        return carry

    lax.fori_loop(ng - mine, ng, send_b, 0)

    lane = lax.broadcasted_iota(jnp.int32, (tok, lanes), 1)
    first_head = lane < head_dim
    one = lax.broadcasted_iota(jnp.int32, (1, lanes), 1)
    loads[7].wait()
    gains = skipv[...]
    for q in range(NX):
        span = quarter(q)
        gain = jnp.where(one < head_dim, gains[:, 2 * q : 2 * q + 1], gains[:, 2 * q + 1 : 2 * q + 2])
        xq = acc[:, span]
        xb = xq.astype(BF16)
        y_loc[:, span] = (
            jnp.where(first_head, dot(wts[2 * q], xb), dot(wts[2 * q + 1], xb)) + gain * xq
        )
        gq = grad_y[:, span]
        gb = gq.astype(BF16)
        gx_loc[:, span] = (
            jnp.where(first_head, dot(wts_t[2 * q], gb), dot(wts_t[2 * q + 1], gb)) + gain * gq
        )

    for d in range(1, ng):
        links.arrive(k_tg + d, groups.at[at_g(ng - d)], dev_g(d))

    def join(i, carry):
        return jnp.exp(groups[i, 0:1, :]) * carry + t_g[i].astype(F32)

    def from_earlier(i, carry):
        links.arrive(k_g + mine - i, t_g.at[i], dev_g(1))
        return join(i, carry)

    carry = lax.fori_loop(0, mine, from_earlier, nothing())
    fall = jnp.ones((1, lanes), F32)
    for i in range(NG):
        f_back[i] = (f_pre[i] + fall * carry).astype(BF16)
        fall = fall * fall_of(i)
    k_bf = new(NG)
    for d in range(1, NG):
        links.send(k_bf + d, f_back.at[at_m(d)], f_in.at[me], dev_m(d))
    f_in[me] = f_back[me]

    def from_later(i, carry):
        source = ng - 1 - i
        links.arrive(k_g + ng + mine - source, t_g.at[source], dev_g(1))
        return join(source, carry)

    carry = lax.fori_loop(0, ng - 1 - mine, from_later, nothing())
    fall = jnp.ones((1, lanes), F32)
    for i in reversed(range(NG)):
        b_back[i] = (b_pre[i] + fall * carry).astype(BF16)
        fall = fall * fall_of(i)
    k_bb = new(NG)
    for d in range(1, NG):
        links.send(k_bb + d, b_back.at[at_m(d)], b_in.at[me], dev_m(d))
    b_in[me] = b_back[me]

    def whole(pieces, q):
        return jnp.concatenate([pieces[q + p * NX] for p in range(NP)], axis=0)

    b_all, c_all = bv[...].astype(BF16), cv[...].astype(BF16)
    for d in range(1, NG):
        links.arrive(k_bf + d, f_in.at[at_m(NG - d)], dev_m(d))
    entered = jnp.concatenate([whole(f_in, q) for q in range(NX)], axis=1)
    out_y = y_loc[...] + dec_in[...] * dot(c_all, entered)
    gz[...] = (fz[...] * out_y).astype(BF16)
    for i, blk in enumerate((blk_o + other, blk_o)):
        for h in HALVES:
            early[2 * i + h] = dot_t(gz[...], wz[blk, h * half : (h + 1) * half, :])
    for d in range(1, NG):
        links.arrive(k_bb + d, b_in.at[at_m(NG - d)], dev_m(d))
    entered = jnp.concatenate([whole(b_in, q) for q in range(NX)], axis=1)
    gx[...] = (gx_loc[...] + dec_out[...] * dot(b_all, entered)).astype(BF16)

    def share(blk, h, done):
        span = slice(h * half, (h + 1) * half)
        from_z = dot_t(gz[...], wz[blk, span, :]) if done is None else early[done + h]
        return dot_t(gx[...], wx[blk, span, :]) + from_z

    k_rs = new(8)

    def to_sib(slot, blk, h, done=None):
        s_sib[slot, h] = share(blk + other, h, done).astype(BF16)
        links.send(k_rs + 2 * slot + h, s_sib.at[slot, h], r_sib.at[slot, h], sib)

    def both(slot, blk, h, done=None):
        own = share(blk, h, done)
        links.arrive(k_rs + 2 * slot + h, r_sib.at[slot, h], sib)
        return own + r_sib[slot, h].astype(F32)

    k_or, k_ol = new(2), new(2)
    k_er, k_el = new(3), new(3)
    parts = [pl.ds(i * (tok // 2), tok // 2) for i in range(2)]
    to_sib(0, blk_o, LO, 0)
    to_sib(0, blk_o, HI, 0)
    to_sib(1, blk_r, HI)
    to_sib(2, blk_l, LO)
    cs_opp[LO] = both(0, blk_o, LO, 2).astype(BF16)
    for i, rows in enumerate(parts):
        links.send(k_or + i, cs_opp.at[LO, rows], r_opp.at[LO, rows], right)
    cs_opp[HI] = both(0, blk_o, HI, 2).astype(BF16)
    for i, rows in enumerate(parts):
        links.send(k_ol + i, cs_opp.at[HI, rows], r_opp.at[HI, rows], left)
    s_right[HI] = both(1, blk_r, HI).astype(BF16)
    links.send(k_er + 2, s_right.at[HI], r_left.at[HI], right)
    s_left[LO] = both(2, blk_l, LO).astype(BF16)
    links.send(k_el + 2, s_left.at[LO], r_right.at[LO], left)
    to_sib(1, blk_r, LO)
    to_sib(2, blk_l, HI)
    for h in HALVES:
        to_sib(3, head, h)
    cs_r[...] = both(1, blk_r, LO)
    cs_l[...] = both(2, blk_l, HI)
    for i, rows in enumerate(parts):
        links.arrive(k_or + i, r_opp.at[LO, rows], left)
        s_right[LO, rows] = (cs_r[rows, :] + r_opp[LO, rows].astype(F32)).astype(BF16)
        links.send(k_er + i, s_right.at[LO, rows], r_left.at[LO, rows], right)
        links.arrive(k_ol + i, r_opp.at[HI, rows], right)
        s_left[HI, rows] = (cs_l[rows, :] + r_opp[HI, rows].astype(F32)).astype(BF16)
        links.send(k_el + i, s_left.at[HI, rows], r_right.at[HI, rows], left)
    for h in HALVES:
        outv[h] = both(3, head, h)
    links.arrive(k_el + 2, r_right.at[LO], right)
    outv[LO] = outv[LO] + r_right[LO].astype(F32)
    links.arrive(k_er + 2, r_left.at[HI], left)
    outv[HI] = outv[HI] + r_left[HI].astype(F32)
    for i, rows in enumerate(parts):
        links.arrive(k_er + i, r_left.at[LO, rows], left)
        out[rows, :half] = outv[LO, rows] + r_left[LO, rows].astype(F32)
        links.arrive(k_el + i, r_right.at[HI, rows], right)
        out[rows, half:] = outv[HI, rows] + r_right[HI, rows].astype(F32)

    def sent_f(d, carry):
        links.make(k_g + d, f_tot, f_tot, dev_g(1)).wait_send()
        return carry

    lax.fori_loop(1, ng, sent_f, 0)
    links.finish()


SEMS = 96


def local(
    embedding,
    noise_draw,
    weight_x,
    weight_z,
    b_proj,
    c_proj,
    log_decay,
    skip_gain,
    class_weight,
    true_label,
):
    tok, feat = embedding.shape
    width = weight_x.shape[1]
    heads = skip_gain.shape[0]
    state = b_proj.shape[1]
    classes = class_weight.shape[1]
    n_head = lax.axis_size("head")
    nz = lax.axis_size("seq") // NX
    ny = n_head // 2
    lanes = width // NX
    half = feat // 2
    vm = pltpu.VMEM
    halves = [vm((2, tok, half), BF16)] * 2
    rows = state // NP
    eighths = [vm((NG, rows, lanes), BF16)] * 2
    scratch = [
        vm((tok, feat), BF16),
        vm((tok, feat), BF16),
        vm((n_head, feat, width), BF16),
        vm((n_head, feat, width), BF16),
        vm((tok, state), F32),
        vm((tok, state), F32),
        vm((heads, tok), F32),
        vm((classes, width), BF16),
        vm((1, tok), jnp.int32),
        vm((1, heads), F32),
        vm((n_head, 2, tok, half), BF16),
        vm((tok, 2 * width), F32),
        vm((tok, width), F32),
        vm((tok, width), F32),
        vm((tok, width), F32),
        vm((heads, tok, tok), BF16),
        vm((heads, tok, tok), BF16),
        vm((state, tok), BF16),
        vm((state, tok), BF16),
        vm((NX, 8, lanes), F32),
        vm((NG, 8, lanes), F32),
        vm((8, lanes), F32),
        vm((nz // NP, 8, lanes), F32),
        *eighths,
        *eighths,
        vm((NG, rows, lanes), F32),
        vm((NG, rows, lanes), F32),
        vm((rows, lanes), BF16),
        vm((rows, lanes), BF16),
        vm((nz // NP, rows, lanes), BF16),
        *eighths,
        *eighths,
        vm((tok, width), F32),
        vm((tok, width), F32),
        vm((tok, width), F32),
        vm((tok, width), BF16),
        vm((tok, width), BF16),
        vm((4, 2, tok, half), BF16),
        vm((4, 2, tok, half), BF16),
        *halves,
        vm((tok, half), F32),
        vm((tok, half), F32),
        *halves,
        *halves,
        vm((2, tok, half), F32),
        vm((4, tok, half), F32),
        pltpu.SemaphoreType.DMA((10,)),
        pltpu.SemaphoreType.REGULAR((3,)),
        pltpu.SemaphoreType.DMA((SEMS,)),
        pltpu.SemaphoreType.DMA((SEMS,)),
    ]
    anywhere = pl.BlockSpec(memory_space=pl.ANY)
    return pl.pallas_call(
        functools.partial(kernel, nz, ny),
        out_shape=pltpu.VMEM((tok, feat), F32),
        in_specs=[anywhere] * 10,
        out_specs=pl.BlockSpec(memory_space=pltpu.VMEM),
        scratch_shapes=scratch,
        compiler_params=pltpu.CompilerParams(
            collective_id=0, has_side_effects=True, vmem_limit_bytes=60 * 1024 * 1024
        ),
        cost_estimate=pl.CostEstimate(
            flops=8 * tok * feat * n_head * width,
            bytes_accessed=10 * 1024 * 1024,
            transcendentals=heads * tok * tok * 2,
        ),
    )(
        embedding,
        noise_draw,
        weight_x.reshape(n_head, feat, width),
        weight_z.reshape(n_head, feat, width),
        b_proj,
        c_proj,
        log_decay,
        class_weight.T,
        true_label.reshape(1, tok),
        skip_gain.reshape(1, heads),
    )


def solution(mesh):
    return jax.shard_map(
        local,
        mesh=mesh,
        in_specs=(
            P("seq", "head"),
            P("seq", "head"),
            P(None, "head"),
            P(None, "head"),
            P("seq", None),
            P("seq", None),
            P("head", "seq"),
            P("head"),
            P("head", None),
            P("seq"),
        ),
        out_specs=P("seq", "head"),
        check_vma=False,
    )
```

```python
import functools

import jax
import jax.numpy as jnp
from jax import lax
from jax.experimental import pallas as pl
from jax.experimental.pallas import tpu as pltpu
from jax.sharding import PartitionSpec as P

F32 = jnp.float32
BF16 = jnp.bfloat16
MESH = pl.DeviceIdType.MESH
NX = 4
NP = 2
NG = NP * NX
PRECISE = lax.Precision.HIGHEST
LO, HI = 0, 1
HALVES = (LO, HI)


def dot(a, b):
    return jnp.dot(a, b, preferred_element_type=F32)


def dot_t(a, b, precision=None):
    return lax.dot_general(
        a, b, (((1,), (1,)), ((), ())), preferred_element_type=F32, precision=precision
    )


class Links:
    def __init__(self, send_sems, recv_sems):
        self.send_sems, self.recv_sems = send_sems, recv_sems
        self.sent = []

    def make(self, k, src, dst, device):
        return pltpu.make_async_remote_copy(
            src_ref=src,
            dst_ref=dst,
            send_sem=self.send_sems.at[k],
            recv_sem=self.recv_sems.at[k],
            device_id=device,
            device_id_type=MESH,
        )

    def send(self, k, src, dst, device):
        copy = self.make(k, src, dst, device)
        copy.start()
        self.sent.append(copy)

    def arrive(self, k, dst, device):
        self.make(k, dst, dst, device).wait_recv()

    def finish(self):
        for copy in self.sent:
            copy.wait_send()


def kernel(
    nz,
    ny,
    emb_h,
    noise_h,
    wx_h,
    wz_h,
    b_h,
    c_h,
    ld_h,
    cw_h,
    lab_h,
    skip_h,
    out,
    ev,
    nv,
    wx,
    wz,
    bv,
    cv,
    ldv,
    cwv,
    labv,
    skipv,
    mix,
    acc,
    dec_in,
    dec_out,
    cols,
    wts,
    wts_t,
    b_t,
    c_t,
    tots,
    tots_m,
    group,
    groups,
    f_send,
    b_send,
    f_x,
    b_x,
    f_pre,
    b_pre,
    f_tot,
    b_tot,
    t_g,
    f_back,
    b_back,
    f_in,
    b_in,
    y_loc,
    gx_loc,
    fz,
    gx,
    gz,
    s_sib,
    r_sib,
    cs_opp,
    r_opp,
    cs_r,
    cs_l,
    s_right,
    s_left,
    r_left,
    r_right,
    outv,
    early,
    local_sems,
    relay,
    send_sems,
    recv_sems,
):
    tok, feat = ev.shape
    half = feat // 2
    width = acc.shape[1] // 2
    heads = ldv.shape[0]
    head_dim = width // heads
    state = bv.shape[1]
    lanes = width // NX
    seq, head = lax.axis_index("seq"), lax.axis_index("head")
    z, x = seq // NX, seq % NX
    y, core = head // 2, head % 2
    other = 1 - 2 * core

    links = Links(send_sems, recv_sems)
    counter = [0]

    def new(count=1):
        first = counter[0]
        counter[0] += count
        return first

    pairs = [
        (emb_h, ev),
        (noise_h, nv),
        (ld_h, ldv),
        (b_h, bv),
        (c_h, cv),
        (cw_h, cwv),
        (lab_h, labv),
        (skip_h, skipv),
        (wx_h, wx),
        (wz_h, wz),
    ]
    loads = [pltpu.make_async_copy(s, d, local_sems.at[i]) for i, (s, d) in enumerate(pairs)]
    for load in loads:
        load.start()

    sib = {"head": head + other}
    blk_r = ((y + 1) % ny) * 2 + core
    blk_l = ((y + ny - 1) % ny) * 2 + core
    blk_o = ((y + 2) % ny) * 2 + core
    right, left = {"head": blk_r}, {"head": blk_l}

    ng = nz // NP
    me, mine = (z % NP) * NX + x, z // NP

    def at_m(d):
        return (me + d) % NG

    def at_g(d):
        return (mine + d) % ng

    def dev_m(d):
        return {"seq": mine * NG + at_m(d)}

    def dev_g(d):
        return {"seq": at_g(d) * NG + me}

    barrier = pltpu.get_barrier_semaphore()
    near = [{"seq": z * NX + (x + d) % NX} for d in (1, NX - 1)]
    near += [{"seq": (z + d) % nz * NX + x} for d in (1, nz - 1)]
    partners = [sib, right, left] + near
    for partner in partners:
        pl.semaphore_signal(barrier, inc=1, device_id=partner, device_id_type=MESH)

    def tell(r):
        for partner in near:
            pl.semaphore_signal(relay.at[r], inc=1, device_id=partner, device_id_type=MESH)

    def told(r):
        pl.semaphore_wait(relay.at[r], len(near))

    loads[0].wait()
    loads[1].wait()
    noisy = (ev[...].astype(F32) + nv[...].astype(F32)).astype(BF16)
    for h in HALVES:
        mix[head, h] = noisy[:, h * half : (h + 1) * half]
    pl.semaphore_wait(barrier, len(partners))

    def piece(blk, h):
        return mix.at[blk, h]

    k_r, k_l, k_own = new(2), new(2), new()
    k_fr, k_fl = new(), new()
    k_sib = {name: new(2) for name in ("l", "r", "o")}

    def hand_on(name, blk, h):
        links.send(k_sib[name] + h, piece(blk, h), piece(blk, h), sib)

    def from_sib(name, blk, h):
        links.arrive(k_sib[name] + h, piece(blk, h), sib)

    links.send(k_r + LO, piece(head, LO), piece(head, LO), right)
    links.send(k_l + HI, piece(head, HI), piece(head, HI), left)
    links.send(k_own, mix.at[head], mix.at[head], sib)
    links.send(k_r + HI, piece(head, HI), piece(head, HI), right)
    links.send(k_l + LO, piece(head, LO), piece(head, LO), left)
    tell(0)

    loads[2].wait()
    rates = ldv[...]
    ones_t = lax.broadcasted_iota(jnp.int32, (tok, tok), 0)
    ones_s = lax.broadcasted_iota(jnp.int32, (tok, tok), 1)
    lower = ones_t >= ones_s
    tri = jnp.where(lower, 1.0, 0.0).astype(F32)
    tri_t = jnp.where(ones_s >= ones_t, 1.0, 0.0).astype(F32)
    cum_row = jnp.dot(rates, tri_t, preferred_element_type=F32, precision=PRECISE)
    wide = jnp.concatenate(
        [jnp.broadcast_to(rates[h : h + 1, :], (head_dim, tok)) for h in range(heads)], axis=0
    )
    cum = dot_t(tri, wide, PRECISE)
    total = cum[tok - 1 : tok, :]
    dec_in[...] = jnp.exp(cum)
    dec_out[...] = jnp.exp(total - cum)
    for q in range(NX):
        tots[q] = jnp.broadcast_to(total[:, q * lanes : (q + 1) * lanes], (8, lanes))
    tots_m[me] = tots[x]
    told(0)
    tell(1)

    links.arrive(k_r + LO, piece(blk_l, LO), left)
    links.send(k_fr, piece(blk_l, LO), piece(blk_l, LO), right)
    hand_on("l", blk_l, LO)
    links.arrive(k_l + HI, piece(blk_r, HI), right)
    links.send(k_fl, piece(blk_r, HI), piece(blk_r, HI), left)
    hand_on("r", blk_r, HI)
    told(1)
    tell(2)
    k_tm = new(NG)
    for d in range(1, NG):
        links.send(k_tm + d, tots.at[at_m(d) % NX], tots_m.at[me], dev_m(d))

    loads[5].wait()
    loads[6].wait()
    classes = cwv.shape[0]
    is_label = lax.broadcasted_iota(jnp.int32, (128, tok), 0) == labv[...]
    onehot = jnp.where(is_label, 1.0, 0.0).astype(F32).T[:, :classes].astype(BF16)
    cols[...] = dot(onehot, cwv[...])

    loads[3].wait()
    loads[4].wait()
    b_all, c_all = bv[...], cv[...]
    scores = dot_t(c_all, b_all, PRECISE)
    scores_t = dot_t(b_all, c_all, PRECISE)
    b_t[...] = b_all.T.astype(BF16)
    c_t[...] = c_all.T.astype(BF16)

    def span_weights(h):
        down = jnp.broadcast_to(cum[:, h * head_dim : h * head_dim + 1], (tok, tok))
        across = jnp.broadcast_to(cum_row[h : h + 1, :], (tok, tok))
        fall = jnp.exp(jnp.minimum(down - across, 0.0))
        wts[h] = (jnp.where(lower, fall, 0.0) * scores).astype(BF16)
        rise = jnp.exp(jnp.minimum(across - down, 0.0))
        wts_t[h] = (jnp.where(ones_s >= ones_t, rise, 0.0) * scores_t).astype(BF16)

    def project(blk, h, first=False):
        m = mix[blk, h]
        for i, w in enumerate((wx, wz)):
            span = slice(i * width, (i + 1) * width)
            term = dot(m, w[blk, h * half : (h + 1) * half, :])
            acc[:, span] = term if first else acc[:, span] + term

    for h in range(0, 2):
        span_weights(h)
    loads[8].wait()
    loads[9].wait()
    project(head, LO, True)
    project(head, HI)

    links.arrive(k_own, mix.at[head + other], sib)
    links.arrive(k_r + HI, piece(blk_l, HI), left)
    hand_on("l", blk_l, HI)
    links.arrive(k_l + LO, piece(blk_r, LO), right)
    hand_on("r", blk_r, LO)
    for h in HALVES:
        project(head + other, h)

    for h in HALVES:
        project(blk_l, h)
        project(blk_r, h)
    for h in HALVES:
        from_sib("l", blk_l + other, h)
        project(blk_l + other, h)
        from_sib("r", blk_r + other, h)
        project(blk_r + other, h)

    links.arrive(k_fr, piece(blk_o, LO), left)
    hand_on("o", blk_o, LO)
    links.arrive(k_fl, piece(blk_o, HI), right)
    hand_on("o", blk_o, HI)
    for h in HALVES:
        project(blk_o, h)
    for h in HALVES:
        from_sib("o", blk_o + other, h)
        project(blk_o + other, h)

    def quarter(q):
        return slice(q * lanes, (q + 1) * lanes)

    xs = acc[:, :width]
    x_end = dot(b_t[...], (xs * dec_out[...]).astype(BF16)).astype(BF16)
    rows = state // NP
    for i in range(NG):
        f_send[i] = x_end[i // NX * rows : (i // NX + 1) * rows, quarter(i % NX)]
    k_ax = new(NG)
    for d in range(1, NG):
        links.send(k_ax + d, f_send.at[at_m(d)], f_x.at[me], dev_m(d))
    f_x[me] = f_send[me]

    zs = acc[:, width:]
    sig = jax.nn.sigmoid(zs)
    grad_y = cols[...] * (zs * sig)
    g_end = dot(c_t[...], (grad_y * dec_in[...]).astype(BF16)).astype(BF16)
    for i in range(NG):
        b_send[i] = g_end[i // NX * rows : (i // NX + 1) * rows, quarter(i % NX)]
    k_ab = new(NG)
    for d in range(1, NG):
        links.send(k_ab + d, b_send.at[at_m(d)], b_x.at[me], dev_m(d))
    b_x[me] = b_send[me]
    fz[...] = cols[...] * sig * (1.0 + zs * (1.0 - sig))
    for d in range(1, NG):
        links.arrive(k_tm + d, tots_m.at[at_m(NG - d)], dev_m(d))
    group[...] = functools.reduce(lambda a, b: a + b, [tots_m[i] for i in range(NG)])
    told(2)
    k_tg = new(ng)
    for d in range(1, ng):
        links.send(k_tg + d, group, groups.at[mine], dev_g(d))
    for h in range(2, heads):
        span_weights(h)

    def fall_of(i):
        return jnp.exp(tots_m[i, 0:1, :])

    def nothing():
        return jnp.zeros((rows, lanes), F32)

    for d in range(1, NG):
        links.arrive(k_ax + d, f_x.at[at_m(NG - d)], dev_m(d))
    run = nothing()
    for i in range(NG):
        f_pre[i] = run
        run = fall_of(i) * run + f_x[i].astype(F32)
    f_tot[...] = run.astype(BF16)
    k_g = new(ng)

    def send_f(d, carry):
        links.make(k_g + d, f_tot, t_g.at[mine], {"seq": (mine + d) * NG + me}).start()
        return carry

    lax.fori_loop(1, ng - mine, send_f, 0)

    for d in range(1, NG):
        links.arrive(k_ab + d, b_x.at[at_m(NG - d)], dev_m(d))
    run = nothing()
    for i in reversed(range(NG)):
        b_pre[i] = run
        run = fall_of(i) * run + b_x[i].astype(F32)
    b_tot[...] = run.astype(BF16)

    def send_b(d, carry):
        links.make(k_g + d, b_tot, t_g.at[mine], {"seq": (mine + d - ng) * NG + me}).start()
        return carry

    lax.fori_loop(ng - mine, ng, send_b, 0)

    lane = lax.broadcasted_iota(jnp.int32, (tok, lanes), 1)
    first_head = lane < head_dim
    one = lax.broadcasted_iota(jnp.int32, (1, lanes), 1)
    loads[7].wait()
    gains = skipv[...]
    for q in range(NX):
        span = quarter(q)
        gain = jnp.where(one < head_dim, gains[:, 2 * q : 2 * q + 1], gains[:, 2 * q + 1 : 2 * q + 2])
        xq = acc[:, span]
        xb = xq.astype(BF16)
        y_loc[:, span] = (
            jnp.where(first_head, dot(wts[2 * q], xb), dot(wts[2 * q + 1], xb)) + gain * xq
        )
        gq = grad_y[:, span]
        gb = gq.astype(BF16)
        gx_loc[:, span] = (
            jnp.where(first_head, dot(wts_t[2 * q], gb), dot(wts_t[2 * q + 1], gb)) + gain * gq
        )

    for d in range(1, ng):
        links.arrive(k_tg + d, groups.at[at_g(ng - d)], dev_g(d))

    def join(i, carry):
        return jnp.exp(groups[i, 0:1, :]) * carry + t_g[i].astype(F32)

    def from_earlier(i, carry):
        links.arrive(k_g + mine - i, t_g.at[i], dev_g(1))
        return join(i, carry)

    carry = lax.fori_loop(0, mine, from_earlier, nothing())
    fall = jnp.ones((1, lanes), F32)
    for i in range(NG):
        f_back[i] = (f_pre[i] + fall * carry).astype(BF16)
        fall = fall * fall_of(i)
    k_bf = new(NG)
    for d in range(1, NG):
        links.send(k_bf + d, f_back.at[at_m(d)], f_in.at[me], dev_m(d))
    f_in[me] = f_back[me]

    def from_later(i, carry):
        source = ng - 1 - i
        links.arrive(k_g + ng + mine - source, t_g.at[source], dev_g(1))
        return join(source, carry)

    carry = lax.fori_loop(0, ng - 1 - mine, from_later, nothing())
    fall = jnp.ones((1, lanes), F32)
    for i in reversed(range(NG)):
        b_back[i] = (b_pre[i] + fall * carry).astype(BF16)
        fall = fall * fall_of(i)
    k_bb = new(NG)
    for d in range(1, NG):
        links.send(k_bb + d, b_back.at[at_m(d)], b_in.at[me], dev_m(d))
    b_in[me] = b_back[me]

    def whole(pieces, q):
        return jnp.concatenate([pieces[q + p * NX] for p in range(NP)], axis=0)

    b_all, c_all = bv[...].astype(BF16), cv[...].astype(BF16)
    for d in range(1, NG):
        links.arrive(k_bf + d, f_in.at[at_m(NG - d)], dev_m(d))
    entered = jnp.concatenate([whole(f_in, q) for q in range(NX)], axis=1)
    out_y = y_loc[...] + dec_in[...] * dot(c_all, entered)
    gz[...] = (fz[...] * out_y).astype(BF16)
    for i, blk in enumerate((blk_o + other, blk_o)):
        for h in HALVES:
            early[2 * i + h] = dot_t(gz[...], wz[blk, h * half : (h + 1) * half, :])
    for d in range(1, NG):
        links.arrive(k_bb + d, b_in.at[at_m(NG - d)], dev_m(d))
    entered = jnp.concatenate([whole(b_in, q) for q in range(NX)], axis=1)
    gx[...] = (gx_loc[...] + dec_out[...] * dot(b_all, entered)).astype(BF16)

    def share(blk, h, done):
        span = slice(h * half, (h + 1) * half)
        from_z = dot_t(gz[...], wz[blk, span, :]) if done is None else early[done + h]
        return dot_t(gx[...], wx[blk, span, :]) + from_z

    k_rs = new(8)

    def to_sib(slot, blk, h, done=None):
        s_sib[slot, h] = share(blk + other, h, done).astype(BF16)
        links.send(k_rs + 2 * slot + h, s_sib.at[slot, h], r_sib.at[slot, h], sib)

    def both(slot, blk, h, done=None):
        own = share(blk, h, done)
        links.arrive(k_rs + 2 * slot + h, r_sib.at[slot, h], sib)
        return own + r_sib[slot, h].astype(F32)

    k_or, k_ol = new(), new()
    k_er, k_el = new(2), new(2)
    to_sib(0, blk_o, LO, 0)
    to_sib(0, blk_o, HI, 0)
    to_sib(1, blk_r, HI)
    to_sib(2, blk_l, LO)
    cs_opp[LO] = both(0, blk_o, LO, 2).astype(BF16)
    links.send(k_or, cs_opp.at[LO], r_opp.at[LO], right)
    cs_opp[HI] = both(0, blk_o, HI, 2).astype(BF16)
    links.send(k_ol, cs_opp.at[HI], r_opp.at[HI], left)
    s_right[HI] = both(1, blk_r, HI).astype(BF16)
    links.send(k_er + HI, s_right.at[HI], r_left.at[HI], right)
    s_left[LO] = both(2, blk_l, LO).astype(BF16)
    links.send(k_el + LO, s_left.at[LO], r_right.at[LO], left)
    to_sib(1, blk_r, LO)
    to_sib(2, blk_l, HI)
    for h in HALVES:
        to_sib(3, head, h)
    cs_r[...] = both(1, blk_r, LO)
    cs_l[...] = both(2, blk_l, HI)
    links.arrive(k_or, r_opp.at[LO], left)
    s_right[LO] = (cs_r[...] + r_opp[LO].astype(F32)).astype(BF16)
    links.send(k_er + LO, s_right.at[LO], r_left.at[LO], right)
    links.arrive(k_ol, r_opp.at[HI], right)
    s_left[HI] = (cs_l[...] + r_opp[HI].astype(F32)).astype(BF16)
    links.send(k_el + HI, s_left.at[HI], r_right.at[HI], left)
    for h in HALVES:
        outv[h] = both(3, head, h)
    links.arrive(k_el + LO, r_right.at[LO], right)
    outv[LO] = outv[LO] + r_right[LO].astype(F32)
    links.arrive(k_er + HI, r_left.at[HI], left)
    outv[HI] = outv[HI] + r_left[HI].astype(F32)
    links.arrive(k_er + LO, r_left.at[LO], left)
    out[:, :half] = outv[LO] + r_left[LO].astype(F32)
    links.arrive(k_el + HI, r_right.at[HI], right)
    out[:, half:] = outv[HI] + r_right[HI].astype(F32)

    def sent_f(d, carry):
        links.make(k_g + d, f_tot, f_tot, dev_g(1)).wait_send()
        return carry

    lax.fori_loop(1, ng, sent_f, 0)
    links.finish()


SEMS = 96


def local(
    embedding,
    noise_draw,
    weight_x,
    weight_z,
    b_proj,
    c_proj,
    log_decay,
    skip_gain,
    class_weight,
    true_label,
):
    tok, feat = embedding.shape
    width = weight_x.shape[1]
    heads = skip_gain.shape[0]
    state = b_proj.shape[1]
    classes = class_weight.shape[1]
    n_head = lax.axis_size("head")
    nz = lax.axis_size("seq") // NX
    ny = n_head // 2
    lanes = width // NX
    half = feat // 2
    vm = pltpu.VMEM
    halves = [vm((2, tok, half), BF16)] * 2
    rows = state // NP
    eighths = [vm((NG, rows, lanes), BF16)] * 2
    scratch = [
        vm((tok, feat), BF16),
        vm((tok, feat), BF16),
        vm((n_head, feat, width), BF16),
        vm((n_head, feat, width), BF16),
        vm((tok, state), F32),
        vm((tok, state), F32),
        vm((heads, tok), F32),
        vm((classes, width), BF16),
        vm((1, tok), jnp.int32),
        vm((1, heads), F32),
        vm((n_head, 2, tok, half), BF16),
        vm((tok, 2 * width), F32),
        vm((tok, width), F32),
        vm((tok, width), F32),
        vm((tok, width), F32),
        vm((heads, tok, tok), BF16),
        vm((heads, tok, tok), BF16),
        vm((state, tok), BF16),
        vm((state, tok), BF16),
        vm((NX, 8, lanes), F32),
        vm((NG, 8, lanes), F32),
        vm((8, lanes), F32),
        vm((nz // NP, 8, lanes), F32),
        *eighths,
        *eighths,
        vm((NG, rows, lanes), F32),
        vm((NG, rows, lanes), F32),
        vm((rows, lanes), BF16),
        vm((rows, lanes), BF16),
        vm((nz // NP, rows, lanes), BF16),
        *eighths,
        *eighths,
        vm((tok, width), F32),
        vm((tok, width), F32),
        vm((tok, width), F32),
        vm((tok, width), BF16),
        vm((tok, width), BF16),
        vm((4, 2, tok, half), BF16),
        vm((4, 2, tok, half), BF16),
        *halves,
        vm((tok, half), F32),
        vm((tok, half), F32),
        *halves,
        *halves,
        vm((2, tok, half), F32),
        vm((4, tok, half), F32),
        pltpu.SemaphoreType.DMA((10,)),
        pltpu.SemaphoreType.REGULAR((3,)),
        pltpu.SemaphoreType.DMA((SEMS,)),
        pltpu.SemaphoreType.DMA((SEMS,)),
    ]
    anywhere = pl.BlockSpec(memory_space=pl.ANY)
    return pl.pallas_call(
        functools.partial(kernel, nz, ny),
        out_shape=pltpu.VMEM((tok, feat), F32),
        in_specs=[anywhere] * 10,
        out_specs=pl.BlockSpec(memory_space=pltpu.VMEM),
        scratch_shapes=scratch,
        compiler_params=pltpu.CompilerParams(
            collective_id=0, has_side_effects=True, vmem_limit_bytes=60 * 1024 * 1024
        ),
        cost_estimate=pl.CostEstimate(
            flops=8 * tok * feat * n_head * width,
            bytes_accessed=10 * 1024 * 1024,
            transcendentals=heads * tok * tok * 2,
        ),
    )(
        embedding,
        noise_draw,
        weight_x.reshape(n_head, feat, width),
        weight_z.reshape(n_head, feat, width),
        b_proj,
        c_proj,
        log_decay,
        class_weight.T,
        true_label.reshape(1, tok),
        skip_gain.reshape(1, heads),
    )


def solution(mesh):
    return jax.shard_map(
        local,
        mesh=mesh,
        in_specs=(
            P("seq", "head"),
            P("seq", "head"),
            P(None, "head"),
            P(None, "head"),
            P("seq", None),
            P("seq", None),
            P("head", "seq"),
            P("head"),
            P("head", None),
            P("seq"),
        ),
        out_specs=P("seq", "head"),
        check_vma=False,
    )
```
